32 devices in a mesh: replica: 8 (over z, x), pipe: 2 (over core), tensor: 2 (over y).
Axes of the slice: x: 2, y: 2, z: 4, core: 2. Of those that a mesh axis runs over, the one named last changes fastest.
Arguments:
- patches: bfloat16 [96, 4, 32, 1280], P('replica', 'pipe', None, 'tensor'), may hold values from -6 to 6
- tile_counts: int32 [96], replicated, may hold values from 1 to 4
- ln_gain: float32 [1280], replicated, may hold values from 0.1 to 1.9
- enc_qkv: bfloat16 [1280, 3, 1280], P(None, None, 'tensor'), may hold values from -0.15625 to 0.15625
- enc_out_w: bfloat16 [1280, 1280], P('tensor'), may hold values from -0.15625 to 0.15625
- proj_w: bfloat16 [1280, 8192], P(None, 'tensor'), may hold values from -0.15625 to 0.15625
- cross_kv_w: bfloat16 [8192, 2, 1024], P('tensor'), may hold values from -0.09375 to 0.09375
- k_gain: float32 [128], replicated, may hold values from 0.1 to 1.9
- plan: int32 [96, 1], replicated, may hold values from 0 to 7; in each aligned block of 12 rows (0 to 11, 12 to 23, ...) at most 2 rows name the same one
- row_pick: int32 [512], P(('replica', 'pipe')), may hold values from 0 to 4095
- q_cross: bfloat16 [2, 512, 8192], P(None, ('replica', 'pipe'), 'tensor'), may hold values from -6 to 6
- q_self: bfloat16 [2, 512, 8192], P(None, ('replica', 'pipe'), 'tensor'), may hold values from -6 to 6
- cache_kv: bfloat16 [512, 32, 2, 1024], P(('replica', 'pipe'), None, None, 'tensor'), may hold values from -6 to 6
- new_kv: bfloat16 [2, 512, 2, 1024], P(None, ('replica', 'pipe'), None, 'tensor'), may hold values from -6 to 6
- kv_len: int32 [512], P(('replica', 'pipe')), may hold values from 1 to 32
Outputs:
- cross_out: bfloat16 [2, 512, 8192], P(None, ('replica', 'pipe'), 'tensor')
- self_out: bfloat16 [2, 512, 8192], P(None, ('replica', 'pipe'), 'tensor')
The draws below stay inside these ranges and needn't reach their ends.
Inputs may be any that keep to these rules, and one draw needn't show every extreme that they name: `plan`: among the 12 images g * 12 to (g + 1) * 12 - 1 of one encoder group at most 2 have one replica, exactly 2 in some group; every replica is named by some image.
All inputs are finite; a program needn't handle non-finite values.
Results may differ from the reference program's by a relative error of at most 0.03.
Values may be sent and summed in bfloat16 or wider, within the bound.
A program may use at most 128 MiB of HBM per device.

```python
import math
import jax
import jax.numpy as jnp
import numpy as np
from jax import lax

DM = 8192
HEADS = 64
KV_HEADS = 8
HD = 128
ENC_W = 1280
ENC_HEADS = 16
TILES = 4
TT = 32
IMGS_REP = 12
CAP = 2
ROWS_DEV = 32
STEPS = 2
LMAX = 32
NIMG = 96
DEC = 512
N_REPLICA = 8
N_PIPE = 2


def set_ends(values, key, least, high):
    longest = values.shape.index(max(values.shape))
    spots = []
    for shift in (0, 1):
        where = [jax.random.randint(jax.random.fold_in(key, axis), (), 0, length) for axis, length in enumerate(values.shape)]
        where[longest] = (where[longest] + shift) % values.shape[longest]
        spots.append(tuple(where))
    return values.at[spots[0]].set(least).at[spots[1]].set(high)


def with_spikes(entries, stream_key, source, target, shards_of, factor):
    def block_of(position):
        return (jnp.arange(entries.shape[position]) // (entries.shape[position] // shards_of)).reshape((-1,) + (1,) * (entries.ndim - 1 - position))

    first = jax.random.permutation(stream_key, shards_of)[block_of(target)]
    second = (block_of(target) + shards_of // 2) % shards_of
    return jnp.where((block_of(source) == first) | (block_of(source) == second), factor * entries, entries)


def level_of(key, dims, cuts, least, largest):
    level, own = 1.0, jax.random.fold_in(key, 6)
    for position, parts in cuts:
        steps = jnp.exp(jax.random.uniform(jax.random.fold_in(own, position), (parts,), jnp.float32, least / len(cuts), largest / len(cuts)))
        level = level * jnp.repeat(steps, dims[position] // parts).reshape([-1 if axis == position else 1 for axis in range(len(dims))])
    return level


def routed_block(rng, own, number, rows, count, top, bound, skew):
    ranking = jax.random.permutation(rng, count)
    crowded, usual = load_shares(count, rows * top, bound, skew, True), load_shares(count, rows * top, bound, skew, False)
    places = jnp.arange(count)

    def named(sizes, offset_by):
        used = int((sizes > 0).sum())
        fixed = max(1, used // 4)
        shifted = fixed + (places - fixed + offset_by * (used - fixed)) % max(1, count - fixed)
        return jnp.zeros((count,), jnp.int32).at[ranking[jnp.where(places < fixed, places, shifted)]].set(jnp.asarray(sizes, jnp.int32))

    sizes = jnp.where(number % 4 == 0, named(crowded, number // 4), named(usual, number - number // 4 - 1))
    mixed = jax.random.permutation(jax.random.fold_in(own, 3), count)
    donor, sink = mixed[0:count // 2 * 2:2], mixed[1:count // 2 * 2:2]
    slack = jnp.minimum(sizes[donor] - 1, bound - sizes[sink]) // 2
    slack = jnp.where((donor == ranking[0]) | (sink == ranking[0]) | (sizes[sink] == 0), 0, jnp.maximum(slack, 0))
    shifted = jax.random.randint(jax.random.fold_in(own, 4), (count // 2,), 0, 1 << 20) % (slack + 1)
    sizes = sizes.at[donor].add(-shifted).at[sink].add(shifted)
    labels = jnp.searchsorted(jnp.cumsum(sizes), jnp.arange(rows * top), side="right").astype(jnp.int32)
    listing = labels.reshape(top, rows).T
    listing = listing[jax.random.permutation(jax.random.fold_in(own, 1), rows)]
    offset_by = jax.random.randint(jax.random.fold_in(own, 2), (rows, 1), 0, top)
    return jnp.take_along_axis(listing, (jnp.arange(top)[None, :] + offset_by) % top, axis=1)


def load_shares(number_of, total, limit, slope, full):
    weights = [(1 << 20) // math.isqrt(grade ** slope) + 1 for grade in range(1, number_of + 1)]
    largest = limit if full else min(limit, max(-(-total // number_of), total * weights[0] // sum(weights)))
    least = 1 if total - largest >= number_of - 1 else 0
    holding, rest = [largest] + [least] * (number_of - 1), total - largest - least * (number_of - 1)
    while rest > 0:
        candidates = [i for i in range(1, number_of) if holding[i] < largest] or [i for i in range(1, number_of) if holding[i] < limit]
        pool, budget = sum([weights[i] for i in candidates]), rest
        for i in candidates:
            extra = min(limit - holding[i], max(1, budget * weights[i] // pool), rest)
            holding[i] = holding[i] + extra
            rest = rest - extra
    return np.array(holding)


def noise(stream_key, dims, deviation, limit, cuts=(), kind=jnp.bfloat16):
    values = deviation * jax.random.normal(stream_key, dims, jnp.float32)
    if cuts:
        values = values * level_of(stream_key, dims, cuts, -0.22, 0.18)
    return jnp.clip(values, -limit, limit).astype(kind)


def heavy_noise(stream_key, shape, deviation, most, cuts, heavy, kind=jnp.bfloat16):
    values = deviation * jax.random.normal(stream_key, shape, jnp.float32)
    if cuts:
        values = values * level_of(stream_key, shape, cuts, -0.22, 0.18)
    return jnp.clip(with_spikes(values, jax.random.fold_in(stream_key, 3), *heavy), -most, most).astype(kind)


def setup_inputs(seed: int = 0) -> dict:
    key_of = jax.random.split(jax.random.key(seed), 16)
    patches = noise(key_of[0], (NIMG, TILES, TT, ENC_W), 1.0, 6.0, ((0, 8), (1, 2), (3, 2)))
    tile_counts = set_ends(jax.random.randint(key_of[1], (NIMG,), 1, TILES + 1), jax.random.fold_in(key_of[1], 1), 1, TILES).astype(jnp.int32)
    ln_gain = jnp.clip(1.0 + 0.18 * jax.random.normal(key_of[2], (ENC_W,), jnp.float32), 0.1, 1.9)
    enc_qkv = noise(key_of[3], (ENC_W, 3, ENC_W), ENC_W ** -0.5, 0.15625, ((2, 2),))
    enc_out_w = noise(key_of[4], (ENC_W, ENC_W), ENC_W ** -0.5, 0.15625, ((0, 2),))
    proj_w = noise(key_of[5], (ENC_W, DM), ENC_W ** -0.5, 0.15625, ((1, 2),))
    cross_kv_w = heavy_noise(key_of[6], (DM, 2, KV_HEADS * HD), DM ** -0.5, 0.09375, ((0, 2),), (0, 2, 2, 2.0))
    k_gain = jnp.clip(1.0 + 0.18 * jax.random.normal(key_of[7], (HD,), jnp.float32), 0.1, 1.9)
    plan_keys = jax.random.split(jax.random.fold_in(key_of[8], 1), NIMG // IMGS_REP)
    plan_turns = jax.random.permutation(jax.random.fold_in(key_of[8], 3), NIMG // IMGS_REP)
    plan = jax.vmap(lambda own, number: routed_block(jax.random.fold_in(key_of[8], 2), own, number, IMGS_REP, N_REPLICA, 1, CAP, 2))(plan_keys, plan_turns).reshape((NIMG, 1))
    row_pick = set_ends(jax.random.randint(key_of[9], (DEC,), 0, 4096), jax.random.fold_in(key_of[9], 1), 0, 4095).astype(jnp.int32)
    q_cross = noise(key_of[10], (STEPS, DEC, HEADS * HD), 1.0, 6.0, ((1, 16), (2, 2)))
    q_self = noise(key_of[11], (STEPS, DEC, HEADS * HD), 1.0, 6.0, ((1, 16), (2, 2)))
    cache_kv = noise(key_of[12], (DEC, LMAX, 2, KV_HEADS * HD), 1.0, 6.0, ((0, 16), (3, 2)))
    new_kv = noise(key_of[13], (STEPS, DEC, 2, KV_HEADS * HD), 1.0, 6.0, ((1, 16), (3, 2)))
    kv_len = set_ends(jax.random.randint(key_of[14], (DEC,), 1, LMAX + 1), jax.random.fold_in(key_of[14], 1), 1, LMAX).astype(jnp.int32)
    return {"patches": patches, "tile_counts": tile_counts, "ln_gain": ln_gain, "enc_qkv": enc_qkv, "enc_out_w": enc_out_w, "proj_w": proj_w, "cross_kv_w": cross_kv_w, "k_gain": k_gain, "plan": plan, "row_pick": row_pick, "q_cross": q_cross, "q_self": q_self, "cache_kv": cache_kv, "new_kv": new_kv, "kv_len": kv_len}


def norm_rows(values, gain):
    middle = lax.optimization_barrier(jnp.mean(values, -1, keepdims=True))
    centred = values - middle
    spread = lax.optimization_barrier(jnp.mean(centred * centred, -1, keepdims=True))
    return centred * lax.rsqrt(spread + 1e-06) * gain

def attend(query, keys, values, valid):
    scores = jnp.einsum('bkgd,btkd->bkgt', query.astype(jnp.float32), keys.astype(jnp.float32)) * query.shape[-1] ** (-0.5)
    scores = jnp.where(valid[:, None, None, :], scores, -1e+30)
    highest = lax.optimization_barrier(jnp.max(scores, -1, keepdims=True))
    weights = jnp.exp(scores - highest)
    probs = (weights / lax.optimization_barrier(jnp.sum(weights, -1, keepdims=True))).astype(jnp.bfloat16)
    mixed = jnp.einsum('bkgt,btkd->bkgd', probs.astype(jnp.float32), values.astype(jnp.float32))
    return mixed.astype(jnp.bfloat16)

def reference(patches, tile_counts, ln_gain, enc_qkv, enc_out_w, proj_w, cross_kv_w, k_gain, plan, row_pick, q_cross, q_self, cache_kv, new_kv, kv_len):
    head_dim = ENC_W // ENC_HEADS
    key_rows = TILES * TT

    def encode(pair):
        image, count = pair
        rows = image.astype(jnp.float32).reshape(key_rows, ENC_W)
        normed = norm_rows(rows, ln_gain).astype(jnp.bfloat16)
        projected = jnp.dot(normed, enc_qkv.reshape(ENC_W, 3 * ENC_W), preferred_element_type=jnp.float32)
        projected = projected.astype(jnp.bfloat16).reshape(key_rows, 3, ENC_HEADS, head_dim)
        valid = jnp.arange(key_rows) // TT < count
        scores = jnp.einsum('qhd,khd->hqk', projected[:, 0].astype(jnp.float32), projected[:, 1].astype(jnp.float32)) * head_dim ** (-0.5)
        scores = jnp.where(valid[None, None, :], scores, -1e+30)
        highest = lax.optimization_barrier(jnp.max(scores, -1, keepdims=True))
        weights = jnp.exp(scores - highest)
        probs = (weights / lax.optimization_barrier(jnp.sum(weights, -1, keepdims=True))).astype(jnp.bfloat16)
        mixed = jnp.einsum('hqk,khd->qhd', probs.astype(jnp.float32), projected[:, 2].astype(jnp.float32))
        mixed = mixed.astype(jnp.bfloat16).reshape(key_rows, ENC_W)
        encoded = (rows + jnp.dot(mixed, enc_out_w, preferred_element_type=jnp.float32)).astype(jnp.bfloat16)
        vision = jnp.dot(encoded, proj_w, preferred_element_type=jnp.float32).astype(jnp.bfloat16)
        summed = jnp.dot(vision, cross_kv_w.reshape(DM, 2 * KV_HEADS * HD), preferred_element_type=jnp.float32)
        summed = summed.reshape(key_rows, 2, KV_HEADS, HD)
        key_heads = summed[:, 0]
        key_heads = key_heads * lax.rsqrt(lax.optimization_barrier(jnp.mean(key_heads * key_heads, -1, keepdims=True)) + 1e-05) * k_gain
        return jnp.stack([key_heads, summed[:, 1]], 1).astype(jnp.bfloat16)
    memory = lax.map(encode, (patches, tile_counts))
    destination = plan[:, 0]
    row_group = jnp.arange(DEC) // (ROWS_DEV * N_PIPE)
    mine = (destination[None, :] == row_group[:, None]).astype(jnp.int32)
    count = lax.optimization_barrier(jnp.sum(mine, 1))
    before = jnp.cumsum(mine, 1) - mine
    wanted = row_pick % count
    hit = (mine == 1) & (before == wanted[:, None])
    chosen = lax.optimization_barrier(jnp.sum(jnp.where(hit, jnp.arange(NIMG, dtype=jnp.int32)[None, :], 0), 1)).astype(jnp.int32)
    chosen_counts = tile_counts[chosen]
    blocks = DEC // ROWS_DEV
    group_size = HEADS // KV_HEADS

    def split_rows(array):
        shaped = array.reshape((array.shape[0], blocks, ROWS_DEV) + array.shape[2:])
        return jnp.moveaxis(shaped, 1, 0)

    def decode(pieces):
        cross_q, self_q, cache, fresh_all, lengths, picks, counts_here = pieces
        memory_rows = memory[picks]
        valid_cross = (jnp.arange(key_rows) // TT)[None, :] < counts_here[:, None]
        cache_valid = jnp.arange(LMAX)[None, :] < lengths[:, None]
        cross_list = []
        self_list = []
        for step_index in range(STEPS):
            query = cross_q[step_index].reshape(ROWS_DEV, KV_HEADS, group_size, HD)
            result = attend(query, memory_rows[:, :, 0], memory_rows[:, :, 1], valid_cross)
            cross_list.append(result.reshape(ROWS_DEV, HEADS * HD))
            fresh = jnp.moveaxis(fresh_all[:step_index + 1], 0, 1)
            joined = jnp.concatenate([cache, fresh], 1).reshape(ROWS_DEV, LMAX + step_index + 1, 2, KV_HEADS, HD)
            valid_self = jnp.concatenate([cache_valid, jnp.ones((ROWS_DEV, step_index + 1), bool)], 1)
            query = self_q[step_index].reshape(ROWS_DEV, KV_HEADS, group_size, HD)
            result = attend(query, joined[:, :, 0], joined[:, :, 1], valid_self)
            self_list.append(result.reshape(ROWS_DEV, HEADS * HD))
        return (jnp.stack(cross_list), jnp.stack(self_list))
    pieces = (split_rows(q_cross), split_rows(q_self), cache_kv.reshape((blocks, ROWS_DEV) + cache_kv.shape[1:]), split_rows(new_kv), kv_len.reshape(blocks, ROWS_DEV), chosen.reshape(blocks, ROWS_DEV), chosen_counts.reshape(blocks, ROWS_DEV))
    cross_blocks, self_blocks = lax.map(decode, pieces)
    cross_out = jnp.moveaxis(cross_blocks, 0, 1).reshape(STEPS, DEC, HEADS * HD)
    self_out = jnp.moveaxis(self_blocks, 0, 1).reshape(STEPS, DEC, HEADS * HD)
    return (cross_out, self_out)
```

```python
import functools
import jax
import jax.numpy as jnp
from jax import lax
from jax.experimental import pallas as pl
from jax.experimental.pallas import tpu as pltpu
from jax.sharding import PartitionSpec as P

HEADS = 64
KV_HEADS = 8
HD = 128
ENC_W = 1280
ENC_HEADS = 16
CAP = 2
STEPS = 2
LMAX = 32
COL_PARTS = 4
NT = (((1,), (1,)), ((), ()))
VMEM_LIMIT = 48 * 1024 * 1024


def softmax_rows(scores):
    highest = jnp.max(scores, -1, keepdims=True)
    weights = jnp.exp(scores - highest)
    return (weights / jnp.sum(weights, -1, keepdims=True)).astype(jnp.bfloat16)


def encoder_kernel(head_dim, local_heads, tile_rows, per_step, counts_ref, q_ref, kv_ref, out_ref):
    pipes, _, rows, _ = kv_ref.shape
    width = local_heads * head_dim
    keys = pipes * rows
    step = pl.program_id(0)
    lane = lax.broadcasted_iota(jnp.int32, (1, width), 1)
    key_tile = lax.broadcasted_iota(jnp.int32, (1, keys), 1) // tile_rows
    for s in range(per_step):
        valid = key_tile < counts_ref[step * per_step + s]
        parts = [None] * (-(-width // 128))
        for h in range(local_heads):
            first = h * head_dim // 128
            last = -(-(h + 1) * head_dim // 128)
            low, high = first * 128, min(last * 128, width)
            own = (lane[:, low:high] >= h * head_dim) & (lane[:, low:high] < (h + 1) * head_dim)
            query = jnp.where(own, q_ref[s, :, low:high], jnp.zeros((), jnp.bfloat16))
            key = kv_ref[:, s, :, low:high].reshape(keys, high - low)
            value = kv_ref[:, s, :, width + low : width + high].reshape(keys, high - low)
            scores = lax.dot_general(query, key, NT, preferred_element_type=jnp.float32)
            scores = jnp.where(valid, scores * head_dim ** (-0.5), -1e30)
            mixed = jnp.dot(softmax_rows(scores), value, preferred_element_type=jnp.float32)
            mixed = jnp.where(own, mixed, 0.0)
            for part in range(first, last):
                piece = mixed[:, part * 128 - low : min((part + 1) * 128 - low, high - low)]
                parts[part] = piece if parts[part] is None else parts[part] + piece
        for part, piece in enumerate(parts):
            out_ref[s, :, part * 128 : part * 128 + piece.shape[1]] = piece.astype(jnp.bfloat16)


def encoder_attention(queries, pairs, counts, head_dim, local_heads, tile_rows):
    slots, rows, width = queries.shape
    pipes = pairs.shape[0]
    per_step = 2
    return pl.pallas_call(
        functools.partial(encoder_kernel, head_dim, local_heads, tile_rows, per_step),
        grid_spec=pltpu.PrefetchScalarGridSpec(
            num_scalar_prefetch=1,
            grid=(slots // per_step,),
            in_specs=[
                pl.BlockSpec((per_step, rows, width), lambda i, c: (i, 0, 0)),
                pl.BlockSpec((pipes, per_step, rows, 2 * width), lambda i, c: (0, i, 0, 0)),
            ],
            out_specs=pl.BlockSpec((per_step, rows, width), lambda i, c: (i, 0, 0)),
        ),
        out_shape=jax.ShapeDtypeStruct((slots, rows, width), jnp.bfloat16),
        compiler_params=pltpu.CompilerParams(vmem_limit_bytes=VMEM_LIMIT),
        cost_estimate=pl.CostEstimate(
            flops=16 * slots * local_heads * rows * pipes * rows * 128,
            bytes_accessed=slots * rows * width * 8,
            transcendentals=slots * local_heads * rows * pipes * rows,
        ),
    )(counts, queries, pairs)


def decode_row(query_ref, row, out_ref, keys, values, valid, kv_local):
    scores = jnp.concatenate(
        [
            lax.dot_general(
                query_ref[row, k], keys[:, k * HD : (k + 1) * HD], NT,
                preferred_element_type=jnp.float32,
            )
            for k in range(kv_local)
        ],
        0,
    )
    probs = softmax_rows(jnp.where(valid, scores * HD ** (-0.5), -1e30))
    queries = query_ref.shape[2]
    for k in range(kv_local):
        mixed = jnp.dot(
            probs[k * queries : (k + 1) * queries],
            values[:, k * HD : (k + 1) * HD],
            preferred_element_type=jnp.float32,
        )
        out_ref[row, k] = mixed.astype(jnp.bfloat16)


def cross_kernel(tile_rows, slots_ref, counts_ref, q_ref, kv_ref, out_ref):
    block, kv_local = q_ref.shape[:2]
    pipes, _, rows, both = kv_ref.shape
    keys = pipes * rows
    width = both // 2
    key_tile = lax.broadcasted_iota(jnp.int32, (1, keys), 1) // tile_rows
    for r in range(block):
        at = pl.program_id(0) * block + r
        slot = slots_ref[at]
        valid = key_tile < counts_ref[at]
        held = kv_ref[:, slot].reshape(keys, both)
        decode_row(q_ref, r, out_ref, held[:, :width], held[:, width:], valid, kv_local)


def self_kernel(lengths_ref, q_ref, kv_ref, out_ref):
    block, kv_local, queries, _ = q_ref.shape
    _, keys, both = kv_ref.shape
    width = both // 2
    shape = (kv_local * queries, keys)
    spot = lax.broadcasted_iota(jnp.int32, shape, 1)
    step = lax.broadcasted_iota(jnp.int32, shape, 0) % queries // (queries // STEPS)
    fresh = (spot >= LMAX) & (spot <= LMAX + step)
    for r in range(block):
        valid = fresh | (spot < lengths_ref[pl.program_id(0) * block + r])
        held = kv_ref[r]
        decode_row(q_ref, r, out_ref, held[:, :width], held[:, width:], valid, kv_local)


def cross_attention(queries, memory, slot_ids, counts, tile_rows):
    rows, kv_local, group, _ = queries.shape
    block = 8
    spec = pl.BlockSpec((block, kv_local, group, HD), lambda i, *_: (i, 0, 0, 0))
    keys = memory.shape[0] * memory.shape[2]
    return pl.pallas_call(
        functools.partial(cross_kernel, tile_rows),
        grid_spec=pltpu.PrefetchScalarGridSpec(
            num_scalar_prefetch=2,
            grid=(rows // block,),
            in_specs=[spec, pl.BlockSpec(memory.shape, lambda i, *_: (0, 0, 0, 0))],
            out_specs=spec,
        ),
        out_shape=jax.ShapeDtypeStruct(queries.shape, jnp.bfloat16),
        compiler_params=pltpu.CompilerParams(vmem_limit_bytes=VMEM_LIMIT),
        cost_estimate=pl.CostEstimate(
            flops=16 * rows * kv_local * group * keys * HD,
            bytes_accessed=2 * (memory.size + 2 * queries.size),
            transcendentals=rows * kv_local * group * keys,
        ),
    )(slot_ids, counts, queries, memory)


def self_attention(queries, joined, lengths):
    rows, kv_local, group, _ = queries.shape
    keys, both = joined.shape[1:]
    block = 8
    spec = pl.BlockSpec((block, kv_local, group, HD), lambda i, *_: (i, 0, 0, 0))
    return pl.pallas_call(
        self_kernel,
        grid_spec=pltpu.PrefetchScalarGridSpec(
            num_scalar_prefetch=1,
            grid=(rows // block,),
            in_specs=[spec, pl.BlockSpec((block, keys, both), lambda i, *_: (i, 0, 0))],
            out_specs=spec,
        ),
        out_shape=jax.ShapeDtypeStruct(queries.shape, jnp.bfloat16),
        compiler_params=pltpu.CompilerParams(vmem_limit_bytes=VMEM_LIMIT),
        cost_estimate=pl.CostEstimate(
            flops=16 * rows * kv_local * group * 128 * HD,
            bytes_accessed=2 * (joined.size + 2 * queries.size),
            transcendentals=rows * kv_local * group * keys,
        ),
    )(lengths, queries, joined)


def rows_major(queries, kv_local):
    steps, rows, _ = queries.shape
    shaped = queries.reshape(steps, rows, kv_local, -1, HD)
    return shaped.transpose(1, 2, 0, 3, 4).reshape(rows, kv_local, -1, HD)


def steps_major(mixed):
    rows, kv_local, group, _ = mixed.shape
    shaped = mixed.reshape(rows, kv_local, STEPS, group // STEPS, HD)
    return shaped.transpose(2, 0, 1, 3, 4).reshape(STEPS, rows, -1)


def shards(
    patches,
    tile_counts,
    ln_gain,
    enc_qkv,
    enc_out_w,
    proj_w,
    cross_kv_w,
    k_gain,
    plan,
    row_pick,
    q_cross,
    q_self,
    cache_kv,
    new_kv,
    kv_len,
):
    replicas = lax.axis_size("replica")
    pipes = lax.axis_size("pipe")
    tensors = lax.axis_size("tensor")
    group = lax.axis_index("replica")
    member = group * pipes + lax.axis_index("pipe")
    members = replicas * pipes
    images, held_tiles, tile_rows, width_part = patches.shape
    head_dim = ENC_W // ENC_HEADS
    rows_image = held_tiles * tile_rows
    slots = replicas * CAP
    rows = slots * rows_image
    width = enc_qkv.shape[2]
    local_heads = width // head_dim

    destination = plan[:, 0]
    grouped = destination.reshape(replicas, images)
    earlier = jnp.arange(images)[:, None] < jnp.arange(images)[None, :]
    same_dest = grouped[:, :, None] == grouped[:, None, :]
    ranks = jnp.sum((same_dest & earlier[None]).astype(jnp.int32), 1)
    my_dest = lax.dynamic_index_in_dim(grouped, group, 0, keepdims=False)
    my_rank = lax.dynamic_index_in_dim(ranks, group, 0, keepdims=False)
    selector = (my_dest[None, None, :] == jnp.arange(replicas)[:, None, None]) & (
        my_rank[None, None, :] == jnp.arange(CAP)[None, :, None]
    )
    leaving = jnp.sum(selector * jnp.arange(images)[None, None, :], -1).reshape(-1)
    outgoing = jnp.take(
        patches.reshape(images, rows_image, width_part), leaving, axis=0, mode="clip"
    )
    arrived = lax.all_to_all(
        outgoing.reshape(replicas, CAP * rows_image, width_part),
        "replica", split_axis=0, concat_axis=0, tiled=True,
    ).reshape(rows, width_part)
    whole_rows = lax.all_gather(arrived, "tensor", axis=0)

    row_parts = members // COL_PARTS
    part_rows = ENC_W // row_parts
    kv_width = cross_kv_w.shape[2] // tensors
    part_cols = kv_width // COL_PARTS
    kv_slice = lax.dynamic_slice_in_dim(
        cross_kv_w.reshape(-1, 2, tensors, kv_width), (member % COL_PARTS) * part_cols, part_cols, 3
    )
    proj_slice = lax.dynamic_slice_in_dim(proj_w, (member // COL_PARTS) * part_rows, part_rows, 0)
    kv_slice = kv_slice.transpose(0, 2, 1, 3).reshape(-1, tensors * 2 * part_cols)
    joint = jnp.dot(proj_slice, kv_slice, preferred_element_type=jnp.float32).astype(jnp.bfloat16)
    joint = lax.psum_scatter(joint, "tensor", scatter_dimension=1, tiled=True)
    joint = lax.all_gather(joint, ("replica", "pipe"), axis=0)
    joint = joint.reshape(row_parts, COL_PARTS, part_rows, 2, part_cols)
    joint = joint.transpose(0, 2, 3, 1, 4).reshape(ENC_W, 2 * kv_width)

    out_rows = enc_out_w.shape[0] // members
    out_piece = lax.dynamic_slice_in_dim(enc_out_w, member * out_rows, out_rows, 0)
    out_piece = lax.all_gather(out_piece, "tensor", axis=0)
    out_whole = lax.all_gather(out_piece, ("replica", "pipe"), axis=0)
    out_whole = out_whole.transpose(1, 0, 2, 3).reshape(ENC_W, ENC_W)

    rows_here = row_pick.shape[0]
    kv_local = kv_width // HD
    fresh = new_kv.transpose(1, 0, 2, 3).reshape(rows_here, STEPS, 2 * kv_width)
    joined = jnp.concatenate(
        [
            cache_kv.reshape(rows_here, LMAX, 2 * kv_width),
            fresh,
            jnp.zeros((rows_here, 16 - STEPS, 2 * kv_width), jnp.bfloat16),
        ],
        1,
    )
    self_out = steps_major(self_attention(rows_major(q_self, kv_local), joined, kv_len))

    values = whole_rows.astype(jnp.float32)
    middle = jnp.sum(values, (0, 2), keepdims=True) / ENC_W
    centred = values - middle
    spread = jnp.sum(centred * centred, (0, 2), keepdims=True) / ENC_W
    normed = centred * lax.rsqrt(spread + 1e-06) * ln_gain.reshape(tensors, 1, width_part)
    normed = normed.astype(jnp.bfloat16).transpose(1, 0, 2).reshape(rows, ENC_W)
    projected = jnp.dot(
        normed, enc_qkv.reshape(ENC_W, 3 * width), preferred_element_type=jnp.float32
    ).astype(jnp.bfloat16)
    projected = projected.reshape(slots, rows_image, 3 * width)
    pairs = lax.all_gather(projected[:, :, width:], "pipe", axis=0)
    here = (grouped[:, None, :] == group) & (ranks[:, None, :] == jnp.arange(CAP)[None, :, None])
    slot_counts = jnp.sum(here * tile_counts.reshape(replicas, 1, images), -1).reshape(-1)
    mixed = encoder_attention(
        projected[:, :, :width], pairs, slot_counts.astype(jnp.int32),
        head_dim, local_heads, tile_rows,
    )
    mixed = lax.all_gather(mixed.reshape(rows, width), "tensor", axis=0)
    mixed = mixed.transpose(1, 0, 2).reshape(rows, ENC_W)
    added = jnp.dot(mixed, out_whole, preferred_element_type=jnp.float32)
    residual = whole_rows.transpose(1, 0, 2).reshape(rows, ENC_W).astype(jnp.float32)
    encoded = (residual + added).astype(jnp.bfloat16)
    summed = jnp.dot(encoded, joint, preferred_element_type=jnp.float32)
    key_heads = summed[:, :kv_width].reshape(rows, kv_local, HD)
    key_heads = (
        key_heads * lax.rsqrt(jnp.mean(key_heads * key_heads, -1, keepdims=True) + 1e-05) * k_gain
    )
    packed = jnp.concatenate([key_heads.reshape(rows, kv_width), summed[:, kv_width:]], 1)
    memory = lax.all_gather(
        packed.astype(jnp.bfloat16).reshape(slots, rows_image, 2 * kv_width), "pipe", axis=0
    )

    mine = (destination == group).astype(jnp.int32)
    count = jnp.sum(mine)
    before = jnp.cumsum(mine) - mine
    wanted = row_pick % count
    hit = (mine[None, :] == 1) & (before[None, :] == wanted[:, None])
    index = jnp.arange(replicas * images, dtype=jnp.int32)
    slot_of = index // images * CAP + ranks.reshape(-1)
    slot_ids = jnp.sum(jnp.where(hit, slot_of[None, :], 0), 1).astype(jnp.int32)
    counts_rows = jnp.sum(jnp.where(hit, tile_counts[None, :], 0), 1).astype(jnp.int32)
    cross_out = steps_major(
        cross_attention(rows_major(q_cross, kv_local), memory, slot_ids, counts_rows, tile_rows)
    )
    return (cross_out, self_out)


def solution(mesh):
    in_specs = (
        P("replica", "pipe", None, "tensor"),
        P(),
        P(),
        P(None, None, "tensor"),
        P("tensor", None),
        P(None, "tensor"),
        P("tensor", None, None),
        P(),
        P(),
        P(("replica", "pipe")),
        P(None, ("replica", "pipe"), "tensor"),
        P(None, ("replica", "pipe"), "tensor"),
        P(("replica", "pipe"), None, None, "tensor"),
        P(None, ("replica", "pipe"), None, "tensor"),
        P(("replica", "pipe")),
    )
    out_specs = (P(None, ("replica", "pipe"), "tensor"), P(None, ("replica", "pipe"), "tensor"))
    return jax.shard_map(shards, mesh=mesh, in_specs=in_specs, out_specs=out_specs, check_vma=False)
```

```python
import functools
import jax
import jax.numpy as jnp
from jax import lax
from jax.experimental import pallas as pl
from jax.experimental.pallas import tpu as pltpu
from jax.sharding import PartitionSpec as P

HEADS = 64
KV_HEADS = 8
HD = 128
ENC_W = 1280
ENC_HEADS = 16
CAP = 2
STEPS = 2
LMAX = 32
COL_PARTS = 4
NT = (((1,), (1,)), ((), ()))
VMEM_LIMIT = 48 * 1024 * 1024
MESH = pl.DeviceIdType.MESH


def softmax_rows(scores):
    highest = jnp.max(scores, -1, keepdims=True)
    weights = jnp.exp(scores - highest)
    return (weights / jnp.sum(weights, -1, keepdims=True)).astype(jnp.bfloat16)


def peers_of(axis):
    size = lax.axis_size(axis)
    here = lax.axis_index(axis)
    return [(lax.rem(here + d, size), lax.rem(here + size - d, size)) for d in range(1, size)]


def greet(groups):
    barrier = pltpu.get_barrier_semaphore()
    total = 0
    for axis in groups:
        for target, _ in peers_of(axis):
            pl.semaphore_signal(barrier, inc=1, device_id={axis: target}, device_id_type=MESH)
            total += 1
    pl.semaphore_wait(barrier, total)


def route_kernel(leaving_ref, whole_ref, own_sem, out_send, out_recv, side_send, side_recv):
    group = lax.axis_index("replica")
    side = lax.axis_index("tensor")
    greet(("replica", "tensor"))

    def outward(d, target, block):
        return pltpu.make_async_remote_copy(
            src_ref=leaving_ref.at[target], dst_ref=whole_ref.at[side, block],
            send_sem=out_send.at[d], recv_sem=out_recv.at[d],
            device_id={"replica": target}, device_id_type=MESH,
        )

    def sideways(d, step, source, block, target, owner):
        return pltpu.make_async_remote_copy(
            src_ref=source, dst_ref=whole_ref.at[owner, block],
            send_sem=side_send.at[d, step], recv_sem=side_recv.at[d, step],
            device_id={"tensor": target}, device_id_type=MESH,
        )

    others = peers_of("replica")
    sides = peers_of("tensor")
    order = sorted(range(len(others)), key=lambda d: (min(d, len(others) - 1 - d), d))
    for d, (target, _) in enumerate(sides):
        sideways(d, 0, leaving_ref.at[group], group, target, side).start()
    for d in order:
        outward(d, others[d][0], group).start()
    keep = pltpu.make_async_copy(leaving_ref.at[group], whole_ref.at[side, group], own_sem)
    keep.start()
    for d in order:
        block = others[d][1]
        outward(d, others[d][0], block).wait_recv()
        for e, (target, _) in enumerate(sides):
            sideways(e, d + 1, whole_ref.at[side, block], block, target, side).start()
    keep.wait()
    for d in order:
        outward(d, others[d][0], group).wait_send()
    for e, (target, source) in enumerate(sides):
        for step in range(len(others) + 1):
            block = group if step == 0 else others[step - 1][1]
            copy = sideways(e, step, whole_ref.at[side, block], block, target, source)
            copy.wait_recv()
            copy.wait_send()


def route(leaving):
    replicas = lax.axis_size("replica")
    tensors = lax.axis_size("tensor")
    return pl.pallas_call(
        route_kernel,
        in_specs=[pl.BlockSpec(memory_space=pl.ANY)],
        out_specs=pl.BlockSpec(memory_space=pl.ANY),
        out_shape=jax.ShapeDtypeStruct((tensors,) + leaving.shape, leaving.dtype),
        scratch_shapes=[
            pltpu.SemaphoreType.DMA,
            pltpu.SemaphoreType.DMA((replicas - 1,)),
            pltpu.SemaphoreType.DMA((replicas - 1,)),
            pltpu.SemaphoreType.DMA((tensors - 1, replicas)),
            pltpu.SemaphoreType.DMA((tensors - 1, replicas)),
        ],
        compiler_params=pltpu.CompilerParams(collective_id=0, has_side_effects=True),
    )(leaving)


def encoder_kernel(
    head_dim, local_heads, tile_rows, counts_ref, query_ref, pair_ref, rows_ref, out_w_ref,
    joint_ref, gain_ref, memory_ref, pairs, mixed_all, packed, pair_send, pair_recv, side_send,
    side_recv, last_send, last_recv, own_sem,
):
    pipes, slots, rows, _ = pairs.shape
    tensors = mixed_all.shape[0]
    width = local_heads * head_dim
    keys = pipes * rows
    per_step = 2
    steps = slots // per_step
    wide = 2 * per_step
    wide_steps = slots // wide
    pipe = lax.axis_index("pipe")
    side = lax.axis_index("tensor")
    others = peers_of("pipe")
    sides = peers_of("tensor")
    greet(("pipe", "tensor"))

    def part(step, size):
        return pl.ds(step * size, size)

    def pair_copy(d, step, target):
        return pltpu.make_async_remote_copy(
            src_ref=pair_ref.at[part(step, per_step)],
            dst_ref=pairs.at[pipe, part(step, per_step)],
            send_sem=pair_send.at[d, step], recv_sem=pair_recv.at[d, step],
            device_id={"pipe": target}, device_id_type=MESH,
        )

    def side_copy(d, step, target):
        return pltpu.make_async_remote_copy(
            src_ref=mixed_all.at[side, part(step, per_step)],
            dst_ref=mixed_all.at[side, part(step, per_step)],
            send_sem=side_send.at[d, step], recv_sem=side_recv.at[d, step],
            device_id={"tensor": target}, device_id_type=MESH,
        )

    def last_copy(d, step, target):
        return pltpu.make_async_remote_copy(
            src_ref=packed.at[part(step, wide)],
            dst_ref=memory_ref.at[pipe, part(step, wide)],
            send_sem=last_send.at[d, step], recv_sem=last_recv.at[d, step],
            device_id={"pipe": target}, device_id_type=MESH,
        )

    def own_copy(step):
        return pltpu.make_async_copy(
            packed.at[part(step, wide)], memory_ref.at[pipe, part(step, wide)], own_sem.at[step]
        )

    @pl.loop(0, steps)
    def _(step):
        for d, (target, _) in enumerate(others):
            pair_copy(d, step, target).start()

    lane = lax.broadcasted_iota(jnp.int32, (1, width), 1)
    key_tile = lax.broadcasted_iota(jnp.int32, (1, keys), 1) // tile_rows

    @pl.loop(0, steps)
    def _(step):
        pairs[pipe, part(step, per_step)] = pair_ref[part(step, per_step)]
        for d, (target, _) in enumerate(others):
            pair_copy(d, step, target).wait_recv()
        for s in range(per_step):
            slot = step * per_step + s
            valid = key_tile < counts_ref[slot]
            pieces = [None] * (-(-width // 128))
            for h in range(local_heads):
                first = h * head_dim // 128
                last = -(-(h + 1) * head_dim // 128)
                low, high = first * 128, min(last * 128, width)
                spots = lane[:, low:high]
                own = (spots >= h * head_dim) & (spots < (h + 1) * head_dim)
                query = jnp.where(own, query_ref[slot, :, low:high], jnp.zeros((), jnp.bfloat16))
                key = pairs[:, slot, :, low:high].reshape(keys, high - low)
                value = pairs[:, slot, :, width + low : width + high].reshape(keys, high - low)
                scores = lax.dot_general(query, key, NT, preferred_element_type=jnp.float32)
                scores = jnp.where(valid, scores * head_dim ** (-0.5), -1e30)
                mixed = jnp.dot(softmax_rows(scores), value, preferred_element_type=jnp.float32)
                mixed = jnp.where(own, mixed, 0.0)
                for at in range(first, last):
                    piece = mixed[:, at * 128 - low : min((at + 1) * 128 - low, high - low)]
                    pieces[at] = piece if pieces[at] is None else pieces[at] + piece
            for at, piece in enumerate(pieces):
                mixed_all[side, slot, :, at * 128 : at * 128 + piece.shape[1]] = piece.astype(
                    jnp.bfloat16
                )
        for d, (target, _) in enumerate(sides):
            side_copy(d, step, target).start()

    kv_width = packed.shape[2] // 2

    @pl.loop(0, wide_steps)
    def _(step):
        for d, (target, _) in enumerate(sides):
            for half in range(2):
                side_copy(d, 2 * step + half, target).wait_recv()
        count = wide * rows
        added = rows_ref[part(step, wide)].reshape(count, ENC_W).astype(jnp.float32)
        for t in range(tensors):
            added += jnp.dot(
                mixed_all[t, part(step, wide)].reshape(count, width), out_w_ref[t],
                preferred_element_type=jnp.float32,
            )
        summed = jnp.dot(
            added.astype(jnp.bfloat16), joint_ref[...], preferred_element_type=jnp.float32
        )
        for k in range(kv_width // HD):
            head = summed[:, k * HD : (k + 1) * HD]
            head = head * lax.rsqrt(jnp.mean(head * head, -1, keepdims=True) + 1e-05) * gain_ref[...]
            packed[part(step, wide), :, k * HD : (k + 1) * HD] = head.astype(jnp.bfloat16).reshape(
                wide, rows, HD
            )
        packed[part(step, wide), :, kv_width:] = (
            summed[:, kv_width:].astype(jnp.bfloat16).reshape(wide, rows, kv_width)
        )
        for d, (target, _) in enumerate(others):
            last_copy(d, step, target).start()
        own_copy(step).start()

    @pl.loop(0, steps)
    def _(step):
        for d, (target, _) in enumerate(others):
            pair_copy(d, step, target).wait_send()
        for d, (target, _) in enumerate(sides):
            side_copy(d, step, target).wait_send()

    @pl.loop(0, wide_steps)
    def _(step):
        for d, (target, _) in enumerate(others):
            last_copy(d, step, target).wait_send()
            last_copy(d, step, target).wait_recv()
        own_copy(step).wait()


def encoder(counts, queries, pair, rows, out_w, joint, gain, head_dim, tile_rows):
    slots, rows_image, width = queries.shape
    pipes = lax.axis_size("pipe")
    tensors = lax.axis_size("tensor")
    steps, wide_steps = slots // 2, slots // 4
    both = joint.shape[1]
    vmem = pl.BlockSpec(memory_space=pltpu.VMEM)
    return pl.pallas_call(
        functools.partial(encoder_kernel, head_dim, width // head_dim, tile_rows),
        in_specs=[pl.BlockSpec(memory_space=pltpu.SMEM)] + [vmem] * 6,
        out_specs=pl.BlockSpec(memory_space=pl.ANY),
        out_shape=jax.ShapeDtypeStruct((pipes, slots, rows_image, both), jnp.bfloat16),
        scratch_shapes=[
            pltpu.VMEM((pipes, slots, rows_image, 2 * width), jnp.bfloat16),
            pltpu.VMEM((tensors, slots, rows_image, width), jnp.bfloat16),
            pltpu.VMEM((slots, rows_image, both), jnp.bfloat16),
            pltpu.SemaphoreType.DMA((pipes - 1, steps)),
            pltpu.SemaphoreType.DMA((pipes - 1, steps)),
            pltpu.SemaphoreType.DMA((tensors - 1, steps)),
            pltpu.SemaphoreType.DMA((tensors - 1, steps)),
            pltpu.SemaphoreType.DMA((pipes - 1, wide_steps)),
            pltpu.SemaphoreType.DMA((pipes - 1, wide_steps)),
            pltpu.SemaphoreType.DMA((wide_steps,)),
        ],
        compiler_params=pltpu.CompilerParams(
            collective_id=1, has_side_effects=True, vmem_limit_bytes=VMEM_LIMIT
        ),
    )(counts, queries, pair, rows, out_w, joint, gain)


def decode_row(query_ref, row, out_ref, keys, values, valid, kv_local):
    scores = jnp.concatenate(
        [
            lax.dot_general(
                query_ref[row, k], keys[:, k * HD : (k + 1) * HD], NT,
                preferred_element_type=jnp.float32,
            )
            for k in range(kv_local)
        ],
        0,
    )
    probs = softmax_rows(jnp.where(valid, scores * HD ** (-0.5), -1e30))
    queries = query_ref.shape[2]
    for k in range(kv_local):
        mixed = jnp.dot(
            probs[k * queries : (k + 1) * queries],
            values[:, k * HD : (k + 1) * HD],
            preferred_element_type=jnp.float32,
        )
        out_ref[row, k] = mixed.astype(jnp.bfloat16)


def cross_kernel(tile_rows, slots_ref, counts_ref, q_ref, kv_ref, out_ref):
    block, kv_local = q_ref.shape[:2]
    pipes, _, rows, both = kv_ref.shape
    keys = pipes * rows
    width = both // 2
    key_tile = lax.broadcasted_iota(jnp.int32, (1, keys), 1) // tile_rows
    for r in range(block):
        at = pl.program_id(0) * block + r
        slot = slots_ref[at]
        valid = key_tile < counts_ref[at]
        held = kv_ref[:, slot].reshape(keys, both)
        decode_row(q_ref, r, out_ref, held[:, :width], held[:, width:], valid, kv_local)


def self_kernel(lengths_ref, q_ref, kv_ref, out_ref):
    block, kv_local, queries, _ = q_ref.shape
    _, keys, both = kv_ref.shape
    width = both // 2
    shape = (kv_local * queries, keys)
    spot = lax.broadcasted_iota(jnp.int32, shape, 1)
    step = lax.broadcasted_iota(jnp.int32, shape, 0) % queries // (queries // STEPS)
    fresh = (spot >= LMAX) & (spot <= LMAX + step)
    for r in range(block):
        valid = fresh | (spot < lengths_ref[pl.program_id(0) * block + r])
        held = kv_ref[r]
        decode_row(q_ref, r, out_ref, held[:, :width], held[:, width:], valid, kv_local)


def cross_attention(queries, memory, slot_ids, counts, tile_rows):
    rows, kv_local, group, _ = queries.shape
    block = 8
    spec = pl.BlockSpec((block, kv_local, group, HD), lambda i, *_: (i, 0, 0, 0))
    keys = memory.shape[0] * memory.shape[2]
    return pl.pallas_call(
        functools.partial(cross_kernel, tile_rows),
        grid_spec=pltpu.PrefetchScalarGridSpec(
            num_scalar_prefetch=2,
            grid=(rows // block,),
            in_specs=[spec, pl.BlockSpec(memory.shape, lambda i, *_: (0, 0, 0, 0))],
            out_specs=spec,
        ),
        out_shape=jax.ShapeDtypeStruct(queries.shape, jnp.bfloat16),
        compiler_params=pltpu.CompilerParams(vmem_limit_bytes=VMEM_LIMIT),
        cost_estimate=pl.CostEstimate(
            flops=16 * rows * kv_local * group * keys * HD,
            bytes_accessed=2 * (memory.size + 2 * queries.size),
            transcendentals=rows * kv_local * group * keys,
        ),
    )(slot_ids, counts, queries, memory)


def self_attention(queries, joined, lengths):
    rows, kv_local, group, _ = queries.shape
    keys, both = joined.shape[1:]
    block = 8
    spec = pl.BlockSpec((block, kv_local, group, HD), lambda i, *_: (i, 0, 0, 0))
    return pl.pallas_call(
        self_kernel,
        grid_spec=pltpu.PrefetchScalarGridSpec(
            num_scalar_prefetch=1,
            grid=(rows // block,),
            in_specs=[spec, pl.BlockSpec((block, keys, both), lambda i, *_: (i, 0, 0))],
            out_specs=spec,
        ),
        out_shape=jax.ShapeDtypeStruct(queries.shape, jnp.bfloat16),
        compiler_params=pltpu.CompilerParams(vmem_limit_bytes=VMEM_LIMIT),
        cost_estimate=pl.CostEstimate(
            flops=16 * rows * kv_local * group * 128 * HD,
            bytes_accessed=2 * (joined.size + 2 * queries.size),
            transcendentals=rows * kv_local * group * keys,
        ),
    )(lengths, queries, joined)


def rows_major(queries, kv_local):
    steps, rows, _ = queries.shape
    shaped = queries.reshape(steps, rows, kv_local, -1, HD)
    return shaped.transpose(1, 2, 0, 3, 4).reshape(rows, kv_local, -1, HD)


def steps_major(mixed):
    rows, kv_local, group, _ = mixed.shape
    shaped = mixed.reshape(rows, kv_local, STEPS, group // STEPS, HD)
    return shaped.transpose(2, 0, 1, 3, 4).reshape(STEPS, rows, -1)


def shards(
    patches,
    tile_counts,
    ln_gain,
    enc_qkv,
    enc_out_w,
    proj_w,
    cross_kv_w,
    k_gain,
    plan,
    row_pick,
    q_cross,
    q_self,
    cache_kv,
    new_kv,
    kv_len,
):
    replicas = lax.axis_size("replica")
    pipes = lax.axis_size("pipe")
    tensors = lax.axis_size("tensor")
    group = lax.axis_index("replica")
    member = group * pipes + lax.axis_index("pipe")
    members = replicas * pipes
    images, held_tiles, tile_rows, width_part = patches.shape
    head_dim = ENC_W // ENC_HEADS
    rows_image = held_tiles * tile_rows
    slots = replicas * CAP
    rows = slots * rows_image
    width = enc_qkv.shape[2]
    local_heads = width // head_dim

    destination = plan[:, 0]
    grouped = destination.reshape(replicas, images)
    earlier = jnp.arange(images)[:, None] < jnp.arange(images)[None, :]
    same_dest = grouped[:, :, None] == grouped[:, None, :]
    ranks = jnp.sum((same_dest & earlier[None]).astype(jnp.int32), 1)
    my_dest = lax.dynamic_index_in_dim(grouped, group, 0, keepdims=False)
    my_rank = lax.dynamic_index_in_dim(ranks, group, 0, keepdims=False)
    selector = (my_dest[None, None, :] == jnp.arange(replicas)[:, None, None]) & (
        my_rank[None, None, :] == jnp.arange(CAP)[None, :, None]
    )
    leaving = jnp.sum(selector * jnp.arange(images)[None, None, :], -1).reshape(-1)
    outgoing = jnp.take(
        patches.reshape(images, rows_image, width_part), leaving, axis=0, mode="clip"
    )
    whole_rows = route(outgoing.reshape(replicas, CAP * rows_image, width_part))
    whole_rows = whole_rows.reshape(tensors, rows, width_part)

    row_parts = members // COL_PARTS
    part_rows = ENC_W // row_parts
    kv_width = cross_kv_w.shape[2] // tensors
    part_cols = kv_width // COL_PARTS
    kv_slice = lax.dynamic_slice_in_dim(
        cross_kv_w.reshape(-1, 2, tensors, kv_width), (member % COL_PARTS) * part_cols, part_cols, 3
    )
    proj_slice = lax.dynamic_slice_in_dim(proj_w, (member // COL_PARTS) * part_rows, part_rows, 0)
    kv_slice = kv_slice.transpose(0, 2, 1, 3).reshape(-1, tensors * 2 * part_cols)
    joint = jnp.dot(proj_slice, kv_slice, preferred_element_type=jnp.float32).astype(jnp.bfloat16)
    joint = lax.psum_scatter(joint, "tensor", scatter_dimension=1, tiled=True)
    joint = lax.all_gather(joint, ("replica", "pipe"), axis=0)
    joint = joint.reshape(row_parts, COL_PARTS, part_rows, 2, part_cols)
    joint = joint.transpose(0, 2, 3, 1, 4).reshape(ENC_W, 2 * kv_width)

    out_rows = enc_out_w.shape[0] // members
    out_piece = lax.dynamic_slice_in_dim(enc_out_w, member * out_rows, out_rows, 0)
    out_piece = lax.all_gather(out_piece, "tensor", axis=0)
    out_whole = lax.all_gather(out_piece, ("replica", "pipe"), axis=0)
    out_whole = out_whole.transpose(1, 0, 2, 3).reshape(tensors, width, ENC_W)

    rows_here = row_pick.shape[0]
    kv_local = kv_width // HD
    fresh = new_kv.transpose(1, 0, 2, 3).reshape(rows_here, STEPS, 2 * kv_width)
    joined = jnp.concatenate(
        [
            cache_kv.reshape(rows_here, LMAX, 2 * kv_width),
            fresh,
            jnp.zeros((rows_here, 16 - STEPS, 2 * kv_width), jnp.bfloat16),
        ],
        1,
    )
    self_out = steps_major(self_attention(rows_major(q_self, kv_local), joined, kv_len))

    values = whole_rows.astype(jnp.float32)
    middle = jnp.sum(values, (0, 2), keepdims=True) / ENC_W
    centred = values - middle
    spread = jnp.sum(centred * centred, (0, 2), keepdims=True) / ENC_W
    normed = centred * lax.rsqrt(spread + 1e-06) * ln_gain.reshape(tensors, 1, width_part)
    normed = normed.astype(jnp.bfloat16).transpose(1, 0, 2).reshape(rows, ENC_W)
    qkv_w = enc_qkv.reshape(ENC_W, 3 * width)
    projected = jnp.dot(normed, qkv_w, preferred_element_type=jnp.float32).astype(jnp.bfloat16)
    queries = projected[:, :width].reshape(slots, rows_image, width)
    pair = projected[:, width:].reshape(slots, rows_image, 2 * width)
    here = (grouped[:, None, :] == group) & (ranks[:, None, :] == jnp.arange(CAP)[None, :, None])
    slot_counts = jnp.sum(here * tile_counts.reshape(replicas, 1, images), -1).reshape(-1)
    residual = whole_rows.transpose(1, 0, 2).reshape(slots, rows_image, ENC_W)
    memory = encoder(
        slot_counts.astype(jnp.int32), queries, pair, residual, out_whole, joint,
        k_gain.reshape(1, HD), head_dim, tile_rows,
    )

    mine = (destination == group).astype(jnp.int32)
    count = jnp.sum(mine)
    before = jnp.cumsum(mine) - mine
    wanted = row_pick % count
    hit = (mine[None, :] == 1) & (before[None, :] == wanted[:, None])
    index = jnp.arange(replicas * images, dtype=jnp.int32)
    slot_of = index // images * CAP + ranks.reshape(-1)
    slot_ids = jnp.sum(jnp.where(hit, slot_of[None, :], 0), 1).astype(jnp.int32)
    counts_rows = jnp.sum(jnp.where(hit, tile_counts[None, :], 0), 1).astype(jnp.int32)
    cross_out = steps_major(
        cross_attention(rows_major(q_cross, kv_local), memory, slot_ids, counts_rows, tile_rows)
    )
    return (cross_out, self_out)


def solution(mesh):
    in_specs = (
        P("replica", "pipe", None, "tensor"),
        P(),
        P(),
        P(None, None, "tensor"),
        P("tensor", None),
        P(None, "tensor"),
        P("tensor", None, None),
        P(),
        P(),
        P(("replica", "pipe")),
        P(None, ("replica", "pipe"), "tensor"),
        P(None, ("replica", "pipe"), "tensor"),
        P(("replica", "pipe"), None, None, "tensor"),
        P(None, ("replica", "pipe"), None, "tensor"),
        P(("replica", "pipe")),
    )
    out_specs = (P(None, ("replica", "pipe"), "tensor"), P(None, ("replica", "pipe"), "tensor"))
    return jax.shard_map(shards, mesh=mesh, in_specs=in_specs, out_specs=out_specs, check_vma=False)
```

```python
import functools
import jax
import jax.numpy as jnp
from jax import lax
from jax.experimental import pallas as pl
from jax.experimental.pallas import tpu as pltpu
from jax.sharding import PartitionSpec as P

HEADS = 64
KV_HEADS = 8
HD = 128
ENC_W = 1280
ENC_HEADS = 16
CAP = 2
STEPS = 2
LMAX = 32
NT = (((1,), (1,)), ((), ()))
VMEM_LIMIT = 48 * 1024 * 1024
MESH = pl.DeviceIdType.MESH


def softmax_rows(scores):
    highest = jnp.max(scores, -1, keepdims=True)
    weights = jnp.exp(scores - highest)
    return (weights / jnp.sum(weights, -1, keepdims=True)).astype(jnp.bfloat16)


def peers_of(axis):
    size = lax.axis_size(axis)
    here = lax.axis_index(axis)
    return [(lax.rem(here + d, size), lax.rem(here + size - d, size)) for d in range(1, size)]


def greet(groups):
    barrier = pltpu.get_barrier_semaphore()
    total = 0
    for axis in groups:
        for target, _ in peers_of(axis):
            pl.semaphore_signal(barrier, inc=1, device_id={axis: target}, device_id_type=MESH)
            total += 1
    pl.semaphore_wait(barrier, total)


def route_kernel(
    leaving_ref, lengths_ref, q_ref, kv_ref, whole_ref, self_ref, own_sem, out_send, out_recv,
    side_send, side_recv,
):
    portion = q_ref.shape[0] // leaving_ref.shape[0]
    group = lax.axis_index("replica")
    side = lax.axis_index("tensor")
    greet(("replica", "tensor"))

    def outward(d, target, block):
        return pltpu.make_async_remote_copy(
            src_ref=leaving_ref.at[target], dst_ref=whole_ref.at[side, block],
            send_sem=out_send.at[d], recv_sem=out_recv.at[d],
            device_id={"replica": target}, device_id_type=MESH,
        )

    def sideways(d, step, source, block, target, owner):
        return pltpu.make_async_remote_copy(
            src_ref=source, dst_ref=whole_ref.at[owner, block],
            send_sem=side_send.at[d, step], recv_sem=side_recv.at[d, step],
            device_id={"tensor": target}, device_id_type=MESH,
        )

    others = peers_of("replica")
    sides = peers_of("tensor")
    order = sorted(range(len(others)), key=lambda d: (min(d, len(others) - 1 - d), d))
    for d, (target, _) in enumerate(sides):
        sideways(d, 0, leaving_ref.at[group], group, target, side).start()
    for d in order:
        outward(d, others[d][0], group).start()
    keep = pltpu.make_async_copy(leaving_ref.at[group], whole_ref.at[side, group], own_sem)
    keep.start()

    def decode(index):
        places = [index * portion + r for r in range(portion)]
        self_rows(places, lengths_ref, q_ref, kv_ref, self_ref)

    decode(0)
    for index, d in enumerate(order):
        decode(index + 1)
        block = others[d][1]
        outward(d, others[d][0], block).wait_recv()
        for e, (target, _) in enumerate(sides):
            sideways(e, d + 1, whole_ref.at[side, block], block, target, side).start()
    keep.wait()
    for d in order:
        outward(d, others[d][0], group).wait_send()
    for e, (target, source) in enumerate(sides):
        for step in range(len(others) + 1):
            block = group if step == 0 else others[step - 1][1]
            copy = sideways(e, step, whole_ref.at[side, block], block, target, source)
            copy.wait_recv()
            copy.wait_send()


def route(leaving, lengths, queries, joined):
    replicas = lax.axis_size("replica")
    tensors = lax.axis_size("tensor")
    vmem = pl.BlockSpec(memory_space=pltpu.VMEM)
    return pl.pallas_call(
        route_kernel,
        in_specs=[
            pl.BlockSpec(memory_space=pl.ANY), pl.BlockSpec(memory_space=pltpu.SMEM), vmem, vmem
        ],
        out_specs=(pl.BlockSpec(memory_space=pl.ANY), vmem),
        out_shape=(
            jax.ShapeDtypeStruct((tensors,) + leaving.shape, leaving.dtype),
            jax.ShapeDtypeStruct(queries.shape, jnp.bfloat16),
        ),
        scratch_shapes=[
            pltpu.SemaphoreType.DMA,
            pltpu.SemaphoreType.DMA((replicas - 1,)),
            pltpu.SemaphoreType.DMA((replicas - 1,)),
            pltpu.SemaphoreType.DMA((tensors - 1, replicas)),
            pltpu.SemaphoreType.DMA((tensors - 1, replicas)),
        ],
        compiler_params=pltpu.CompilerParams(
            collective_id=0, has_side_effects=True, vmem_limit_bytes=VMEM_LIMIT
        ),
    )(leaving, lengths, queries, joined)


def project_kernel(rows_ref, gain_ref, weight_ref, query_ref, pair_ref):
    tensors, _, width = rows_ref.shape
    values = [rows_ref[t].astype(jnp.float32) for t in range(tensors)]
    middle = sum(jnp.sum(value, -1, keepdims=True) for value in values) / ENC_W
    centred = [value - middle for value in values]
    spread = sum(jnp.sum(value * value, -1, keepdims=True) for value in centred) / ENC_W
    scale = lax.rsqrt(spread + 1e-06)
    normed = [(value * scale * gain_ref[t]).astype(jnp.bfloat16) for t, value in enumerate(centred)]
    for j in range(3):
        total = sum(
            jnp.dot(
                value, weight_ref[j, t * width : (t + 1) * width, :],
                preferred_element_type=jnp.float32,
            )
            for t, value in enumerate(normed)
        ).astype(jnp.bfloat16)
        if j == 0:
            query_ref[...] = total
        else:
            pair_ref[j - 1] = total


def project(rows, gain, weight):
    tensors, count, part = rows.shape
    width = weight.shape[2]
    block = 256
    return pl.pallas_call(
        project_kernel,
        grid=(count // block,),
        in_specs=[
            pl.BlockSpec((tensors, block, part), lambda i: (0, i, 0)),
            pl.BlockSpec((tensors, 1, part), lambda i: (0, 0, 0)),
            pl.BlockSpec(weight.shape, lambda i: (0, 0, 0)),
        ],
        out_specs=(
            pl.BlockSpec((block, width), lambda i: (i, 0)),
            pl.BlockSpec((2, block, width), lambda i: (0, i, 0)),
        ),
        out_shape=(
            jax.ShapeDtypeStruct((count, width), jnp.bfloat16),
            jax.ShapeDtypeStruct((2, count, width), jnp.bfloat16),
        ),
        compiler_params=pltpu.CompilerParams(vmem_limit_bytes=VMEM_LIMIT),
        cost_estimate=pl.CostEstimate(
            flops=6 * count * ENC_W * width, bytes_accessed=2 * (3 * rows.size + weight.size),
            transcendentals=0,
        ),
    )(rows, gain, weight)


def joint_kernel(
    members_col, proj_ref, out_w_ref, pieces_ref, out_ref, out_rows_ref, rows, leaving, coming,
    row_sem, send, recv, w_send, w_recv,
):
    part_rows, features = rows.shape
    side = lax.axis_index("tensor")
    member = lax.axis_index("replica") * lax.axis_size("pipe") + lax.axis_index("pipe")
    first = pl.multiple_of(member // members_col * part_rows, 8)
    load = pltpu.make_async_copy(proj_ref.at[pl.ds(first, part_rows)], rows, row_sem)
    load.start()
    sides = peers_of("tensor")
    greet(("tensor",))

    def w_copy(d, target):
        return pltpu.make_async_remote_copy(
            src_ref=out_w_ref, dst_ref=out_rows_ref.at[side],
            send_sem=w_send.at[d], recv_sem=w_recv.at[d],
            device_id={"tensor": target}, device_id_type=MESH,
        )

    def sum_copy(d, target):
        return pltpu.make_async_remote_copy(
            src_ref=leaving.at[d], dst_ref=coming.at[d],
            send_sem=send.at[d], recv_sem=recv.at[d],
            device_id={"tensor": target}, device_id_type=MESH,
        )

    def product(target):
        depth = min(1024, features)
        total = jnp.zeros((part_rows, 2 * HD), jnp.float32)
        for low in range(0, features, depth):
            block = pieces_ref[target, :, low : low + depth]
            total += jnp.dot(
                rows[:, low : low + depth], jnp.concatenate([block[0], block[1]], -1),
                preferred_element_type=jnp.float32,
            )
        return total

    for d, (target, _) in enumerate(sides):
        w_copy(d, target).start()
    out_rows_ref[side] = out_w_ref[...]
    load.wait()
    for d, (target, _) in enumerate(sides):
        leaving[d] = product(target).astype(jnp.bfloat16)
        sum_copy(d, target).start()
    total = product(side)
    for d, (target, _) in enumerate(sides):
        sum_copy(d, target).wait_recv()
        total += coming[d].astype(jnp.float32)
    out_ref[...] = total.astype(jnp.bfloat16)
    for d, (target, _) in enumerate(sides):
        sum_copy(d, target).wait_send()
        w_copy(d, target).wait_send()
        w_copy(d, target).wait_recv()


def joint_block(proj, out_w, pieces, members_col, part_rows):
    tensors, _, features, _ = pieces.shape
    vmem = pl.BlockSpec(memory_space=pltpu.VMEM)
    block = (part_rows, 2 * HD)
    one = pltpu.SemaphoreType.DMA((tensors - 1,))
    return pl.pallas_call(
        functools.partial(joint_kernel, members_col),
        in_specs=[pl.BlockSpec(memory_space=pl.ANY), vmem, vmem],
        out_specs=(vmem, vmem),
        out_shape=(
            jax.ShapeDtypeStruct(block, jnp.bfloat16),
            jax.ShapeDtypeStruct((tensors,) + out_w.shape, jnp.bfloat16),
        ),
        scratch_shapes=[
            pltpu.VMEM((part_rows, features), jnp.bfloat16),
            pltpu.VMEM((tensors - 1,) + block, jnp.bfloat16),
            pltpu.VMEM((tensors - 1,) + block, jnp.bfloat16),
            pltpu.SemaphoreType.DMA, one, one, one, one,
        ],
        compiler_params=pltpu.CompilerParams(
            collective_id=3, has_side_effects=True, vmem_limit_bytes=VMEM_LIMIT
        ),
    )(proj, out_w, pieces)


def encoder_kernel(
    head_dim, local_heads, tile_rows, counts_ref, query_ref, pair_ref, mixed_ref, pairs, mixed,
    pair_send, pair_recv, side_send, side_recv, own_sem,
):
    pipes, _, slots, rows, width = pairs.shape
    keys = pipes * rows
    per_step = 2
    steps = slots // per_step
    pipe = lax.axis_index("pipe")
    side = lax.axis_index("tensor")
    others = peers_of("pipe")
    sides = peers_of("tensor")
    greet(("pipe", "tensor"))

    def part(step):
        return pl.ds(step * per_step, per_step)

    def pair_copy(d, step, target):
        return pltpu.make_async_remote_copy(
            src_ref=pair_ref.at[:, part(step)], dst_ref=pairs.at[pipe, :, part(step)],
            send_sem=pair_send.at[d, step], recv_sem=pair_recv.at[d, step],
            device_id={"pipe": target}, device_id_type=MESH,
        )

    def side_copy(d, step, target):
        return pltpu.make_async_remote_copy(
            src_ref=mixed.at[part(step)], dst_ref=mixed_ref.at[side, part(step)],
            send_sem=side_send.at[d, step], recv_sem=side_recv.at[d, step],
            device_id={"tensor": target}, device_id_type=MESH,
        )

    def own_copy(step):
        return pltpu.make_async_copy(
            mixed.at[part(step)], mixed_ref.at[side, part(step)], own_sem.at[step]
        )

    @pl.loop(0, steps)
    def _(step):
        for d, (target, _) in enumerate(others):
            pair_copy(d, step, target).start()

    lane = lax.broadcasted_iota(jnp.int32, (1, width), 1)
    key_tile = lax.broadcasted_iota(jnp.int32, (1, keys), 1) // tile_rows
    windows = []
    for h in range(0, local_heads, 2):
        low = h * head_dim // 128 * 128
        high = min(-(-(h + 2) * head_dim // 128) * 128, width)
        spots = lane[:, low:high]
        owns = [(spots >= g * head_dim) & (spots < (g + 1) * head_dim) for g in (h, h + 1)]
        windows.append((low, high, owns))

    @pl.loop(0, steps)
    def _(step):
        pairs[pipe, :, part(step)] = pair_ref[:, part(step)]
        for d, (target, _) in enumerate(others):
            pair_copy(d, step, target).wait_recv()
        scores = []
        for s in range(per_step):
            slot = step * per_step + s
            valid = key_tile < counts_ref[slot]
            for low, high, owns in windows:
                plain = query_ref[slot, :, low:high]
                both = [jnp.where(own, plain, jnp.zeros((), jnp.bfloat16)) for own in owns]
                key = pairs[:, 0, slot, :, low:high].reshape(keys, high - low)
                score = lax.dot_general(
                    jnp.concatenate(both, 0), key, NT, preferred_element_type=jnp.float32
                )
                scores.append(jnp.where(valid, score * head_dim ** (-0.5), -1e30))
        probs = [softmax_rows(score) for score in scores]
        results = []
        for s in range(per_step):
            slot = step * per_step + s
            for w, (low, high, _) in enumerate(windows):
                value = pairs[:, 1, slot, :, low:high].reshape(keys, high - low)
                results.append(
                    jnp.dot(
                        probs[s * len(windows) + w], value, preferred_element_type=jnp.float32
                    )
                )
        for s in range(per_step):
            slot = step * per_step + s
            pieces = [None] * (-(-width // 128))
            for w, (low, high, owns) in enumerate(windows):
                result = results[s * len(windows) + w]
                joined = jnp.where(owns[0], result[:rows], jnp.where(owns[1], result[rows:], 0.0))
                for at in range(low // 128, -(-high // 128)):
                    piece = joined[:, at * 128 - low : min((at + 1) * 128, high) - low]
                    pieces[at] = piece if pieces[at] is None else pieces[at] + piece
            for at, piece in enumerate(pieces):
                mixed[slot, :, at * 128 : at * 128 + piece.shape[1]] = piece.astype(jnp.bfloat16)
        for d, (target, _) in enumerate(sides):
            side_copy(d, step, target).start()
        own_copy(step).start()

    @pl.loop(0, steps)
    def _(step):
        for d, (target, _) in enumerate(others):
            pair_copy(d, step, target).wait_send()
        for d, (target, _) in enumerate(sides):
            side_copy(d, step, target).wait_send()
            side_copy(d, step, target).wait_recv()
        own_copy(step).wait()


def encoder(counts, queries, pair, head_dim, tile_rows):
    slots, rows_image, width = queries.shape
    pipes = lax.axis_size("pipe")
    tensors = lax.axis_size("tensor")
    steps = slots // 2
    vmem = pl.BlockSpec(memory_space=pltpu.VMEM)
    return pl.pallas_call(
        functools.partial(encoder_kernel, head_dim, width // head_dim, tile_rows),
        in_specs=[pl.BlockSpec(memory_space=pltpu.SMEM), vmem, vmem],
        out_specs=pl.BlockSpec(memory_space=pl.ANY),
        out_shape=jax.ShapeDtypeStruct((tensors, slots, rows_image, width), jnp.bfloat16),
        scratch_shapes=[
            pltpu.VMEM((pipes,) + pair.shape, jnp.bfloat16),
            pltpu.VMEM(queries.shape, jnp.bfloat16),
            pltpu.SemaphoreType.DMA((pipes - 1, steps)),
            pltpu.SemaphoreType.DMA((pipes - 1, steps)),
            pltpu.SemaphoreType.DMA((tensors - 1, steps)),
            pltpu.SemaphoreType.DMA((tensors - 1, steps)),
            pltpu.SemaphoreType.DMA((steps,)),
        ],
        compiler_params=pltpu.CompilerParams(
            collective_id=1, has_side_effects=True, vmem_limit_bytes=VMEM_LIMIT
        ),
    )(counts, queries, pair)


def memory_kernel(mixed_ref, rows_ref, out_w_ref, joint_ref, gain_ref, memory_ref, packed, last_send, last_recv, own_sem):
    tensors, slots, rows, width = mixed_ref.shape
    col_parts = joint_ref.shape[0]
    kv_width = col_parts * HD
    wide = 4
    steps = slots // wide
    pipe = lax.axis_index("pipe")
    others = peers_of("pipe")
    greet(("pipe",))

    def part(step):
        return pl.ds(step * wide, wide)

    def last_copy(d, step, target):
        return pltpu.make_async_remote_copy(
            src_ref=packed.at[part(step)], dst_ref=memory_ref.at[pipe, part(step)],
            send_sem=last_send.at[d, step], recv_sem=last_recv.at[d, step],
            device_id={"pipe": target}, device_id_type=MESH,
        )

    def own_copy(step):
        return pltpu.make_async_copy(
            packed.at[part(step)], memory_ref.at[pipe, part(step)], own_sem.at[step]
        )

    @pl.loop(0, steps)
    def _(step):
        count = wide * rows
        added = sum(
            jnp.dot(
                mixed_ref[t, part(step)].reshape(count, width), out_w_ref[t],
                preferred_element_type=jnp.float32,
            )
            for t in range(tensors)
        )
        encoded = [
            (
                rows_ref[t, part(step)].reshape(count, width).astype(jnp.float32)
                + added[:, t * width : (t + 1) * width]
            ).astype(jnp.bfloat16)
            for t in range(tensors)
        ]
        for c in range(col_parts):
            summed = sum(
                jnp.dot(
                    encoded[t], joint_ref[c, t * width : (t + 1) * width, :],
                    preferred_element_type=jnp.float32,
                )
                for t in range(tensors)
            )
            head = summed[:, :HD]
            spread = jnp.mean(head * head, -1, keepdims=True)
            head = head * lax.rsqrt(spread + 1e-05) * gain_ref[...]
            low = c * HD
            packed[part(step), :, low : low + HD] = head.astype(jnp.bfloat16).reshape(
                wide, rows, HD
            )
            packed[part(step), :, kv_width + low : kv_width + low + HD] = (
                summed[:, HD:].astype(jnp.bfloat16).reshape(wide, rows, HD)
            )
        for d, (target, _) in enumerate(others):
            last_copy(d, step, target).start()
        own_copy(step).start()

    @pl.loop(0, steps)
    def _(step):
        for d, (target, _) in enumerate(others):
            last_copy(d, step, target).wait_send()
            last_copy(d, step, target).wait_recv()
        own_copy(step).wait()


def memory_of(mixed, rows, out_w, joint, gain):
    _, slots, rows_image, _ = mixed.shape
    pipes = lax.axis_size("pipe")
    steps = slots // 4
    both = 2 * joint.shape[0] * HD
    vmem = pl.BlockSpec(memory_space=pltpu.VMEM)
    return pl.pallas_call(
        memory_kernel,
        in_specs=[vmem] * 5,
        out_specs=pl.BlockSpec(memory_space=pl.ANY),
        out_shape=jax.ShapeDtypeStruct((pipes, slots, rows_image, both), jnp.bfloat16),
        scratch_shapes=[
            pltpu.VMEM((slots, rows_image, both), jnp.bfloat16),
            pltpu.SemaphoreType.DMA((pipes - 1, steps)),
            pltpu.SemaphoreType.DMA((pipes - 1, steps)),
            pltpu.SemaphoreType.DMA((steps,)),
        ],
        compiler_params=pltpu.CompilerParams(
            collective_id=2, has_side_effects=True, vmem_limit_bytes=VMEM_LIMIT
        ),
    )(mixed, rows, out_w, joint, gain)


def decode_rows(query_ref, places, out_ref, held, valids):
    kv_local, queries = query_ref.shape[1:3]
    width = kv_local * HD
    scores = []
    for row, pair, valid in zip(places, held, valids):
        for k in range(kv_local):
            scores.append(
                lax.dot_general(
                    query_ref[row, k], pair[:, k * HD : (k + 1) * HD], NT,
                    preferred_element_type=jnp.float32,
                )
            )
    masked = [
        jnp.where(valids[i // kv_local], piece * HD ** (-0.5), -1e30)
        for i, piece in enumerate(scores)
    ]
    probs = softmax_rows(jnp.concatenate(masked, 0))
    for i, (row, pair) in enumerate(zip(places, held)):
        for k in range(kv_local):
            at = (i * kv_local + k) * queries
            mixed = jnp.dot(
                probs[at : at + queries], pair[:, width + k * HD : width + (k + 1) * HD],
                preferred_element_type=jnp.float32,
            )
            out_ref[row, k] = mixed.astype(jnp.bfloat16)


def cross_kernel(tile_rows, slots_ref, counts_ref, q_ref, kv_ref, out_ref):
    block = q_ref.shape[0]
    pipes, _, rows, both = kv_ref.shape
    keys = pipes * rows
    key_tile = lax.broadcasted_iota(jnp.int32, (1, keys), 1) // tile_rows
    for low in range(0, block, 4):
        places = list(range(low, low + 4))
        spots = [pl.program_id(0) * block + r for r in places]
        held = [kv_ref[:, slots_ref[at]].reshape(keys, both) for at in spots]
        decode_rows(q_ref, places, out_ref, held, [key_tile < counts_ref[at] for at in spots])


def self_rows(places, lengths_ref, q_ref, kv_ref, out_ref):
    queries = q_ref.shape[2]
    shape = (queries, kv_ref.shape[1])
    spot = lax.broadcasted_iota(jnp.int32, shape, 1)
    step = lax.broadcasted_iota(jnp.int32, shape, 0) // (queries // STEPS)
    fresh = (spot >= LMAX) & (spot <= LMAX + step)
    valids = [fresh | (spot < lengths_ref[row]) for row in places]
    decode_rows(q_ref, places, out_ref, [kv_ref[row] for row in places], valids)


def cross_attention(queries, memory, slot_ids, counts, tile_rows):
    rows, kv_local, group, _ = queries.shape
    block = 8
    spec = pl.BlockSpec((block, kv_local, group, HD), lambda i, *_: (i, 0, 0, 0))
    keys = memory.shape[0] * memory.shape[2]
    return pl.pallas_call(
        functools.partial(cross_kernel, tile_rows),
        grid_spec=pltpu.PrefetchScalarGridSpec(
            num_scalar_prefetch=2,
            grid=(rows // block,),
            in_specs=[spec, pl.BlockSpec(memory.shape, lambda i, *_: (0, 0, 0, 0))],
            out_specs=spec,
        ),
        out_shape=jax.ShapeDtypeStruct(queries.shape, jnp.bfloat16),
        compiler_params=pltpu.CompilerParams(vmem_limit_bytes=VMEM_LIMIT),
        cost_estimate=pl.CostEstimate(
            flops=16 * rows * kv_local * group * keys * HD,
            bytes_accessed=2 * (memory.size + 2 * queries.size),
            transcendentals=rows * kv_local * group * keys,
        ),
    )(slot_ids, counts, queries, memory)


def rows_major(queries, kv_local):
    steps, rows, _ = queries.shape
    shaped = queries.reshape(steps, rows, kv_local, -1, HD)
    return shaped.transpose(1, 2, 0, 3, 4).reshape(rows, kv_local, -1, HD)


def steps_major(mixed):
    rows, kv_local, group, _ = mixed.shape
    shaped = mixed.reshape(rows, kv_local, STEPS, group // STEPS, HD)
    return shaped.transpose(2, 0, 1, 3, 4).reshape(STEPS, rows, -1)


def shards(
    patches,
    tile_counts,
    ln_gain,
    enc_qkv,
    enc_out_w,
    proj_w,
    cross_kv_w,
    k_gain,
    plan,
    row_pick,
    q_cross,
    q_self,
    cache_kv,
    new_kv,
    kv_len,
):
    replicas = lax.axis_size("replica")
    pipes = lax.axis_size("pipe")
    tensors = lax.axis_size("tensor")
    group = lax.axis_index("replica")
    member = group * pipes + lax.axis_index("pipe")
    members = replicas * pipes
    images, held_tiles, tile_rows, width_part = patches.shape
    head_dim = ENC_W // ENC_HEADS
    rows_image = held_tiles * tile_rows
    slots = replicas * CAP
    rows = slots * rows_image
    width = enc_qkv.shape[2]
    local_heads = width // head_dim

    destination = plan[:, 0]
    grouped = destination.reshape(replicas, images)
    earlier = jnp.arange(images)[:, None] < jnp.arange(images)[None, :]
    same_dest = grouped[:, :, None] == grouped[:, None, :]
    ranks = jnp.sum((same_dest & earlier[None]).astype(jnp.int32), 1)
    my_dest = lax.dynamic_index_in_dim(grouped, group, 0, keepdims=False)
    my_rank = lax.dynamic_index_in_dim(ranks, group, 0, keepdims=False)
    selector = (my_dest[None, None, :] == jnp.arange(replicas)[:, None, None]) & (
        my_rank[None, None, :] == jnp.arange(CAP)[None, :, None]
    )
    leaving = jnp.sum(selector * jnp.arange(images)[None, None, :], -1).reshape(-1)
    outgoing = jnp.take(
        patches.reshape(images, rows_image, width_part), leaving, axis=0, mode="clip"
    )
    kv_width = cross_kv_w.shape[2] // tensors
    kv_local = kv_width // HD
    row_parts = members // kv_local
    part_rows = ENC_W // row_parts
    pieces = lax.optimization_barrier(
        [
            lax.dynamic_slice_in_dim(
                cross_kv_w, t * kv_width + (member % kv_local) * HD, HD, 2
            )
            for t in range(tensors)
        ]
    )
    out_rows = enc_out_w.shape[0] // members
    out_piece = lax.dynamic_slice_in_dim(enc_out_w, member * out_rows, out_rows, 0)
    joint, out_piece = joint_block(
        proj_w, out_piece, jnp.stack([piece.transpose(1, 0, 2) for piece in pieces]), kv_local,
        part_rows,
    )
    out_whole = lax.all_gather(out_piece, ("replica", "pipe"), axis=0)
    out_whole = out_whole.transpose(1, 0, 2, 3).reshape(tensors, width, ENC_W)
    joint = lax.all_gather(joint, ("replica", "pipe"), axis=0)
    joint = joint.reshape(row_parts, kv_local, part_rows, 2 * HD)
    joint = joint.transpose(1, 0, 2, 3).reshape(kv_local, ENC_W, 2 * HD)

    rows_here = row_pick.shape[0]
    fresh = new_kv.transpose(1, 0, 2, 3).reshape(rows_here, STEPS, 2 * kv_width)
    joined = jnp.concatenate(
        [
            cache_kv.reshape(rows_here, LMAX, 2 * kv_width),
            fresh,
            jnp.zeros((rows_here, 16 - STEPS, 2 * kv_width), jnp.bfloat16),
        ],
        1,
    )
    whole_rows, self_out = route(
        outgoing.reshape(replicas, CAP * rows_image, width_part), kv_len,
        rows_major(q_self, kv_local), joined,
    )
    self_out = steps_major(self_out)

    queries, pair = project(
        whole_rows.reshape(tensors, rows, width_part), ln_gain.reshape(tensors, 1, width_part),
        enc_qkv.transpose(1, 0, 2),
    )
    here = (grouped[:, None, :] == group) & (ranks[:, None, :] == jnp.arange(CAP)[None, :, None])
    slot_counts = jnp.sum(here * tile_counts.reshape(replicas, 1, images), -1).reshape(-1)
    mixed = encoder(
        slot_counts.astype(jnp.int32), queries.reshape(slots, rows_image, width),
        pair.reshape(2, slots, rows_image, width), head_dim, tile_rows,
    )
    memory = memory_of(
        mixed, whole_rows.reshape(tensors, slots, rows_image, width_part), out_whole, joint,
        k_gain.reshape(1, HD),
    )

    mine = (destination == group).astype(jnp.int32)
    count = jnp.sum(mine)
    before = jnp.cumsum(mine) - mine
    wanted = row_pick % count
    hit = (mine[None, :] == 1) & (before[None, :] == wanted[:, None])
    index = jnp.arange(replicas * images, dtype=jnp.int32)
    slot_of = index // images * CAP + ranks.reshape(-1)
    slot_ids = jnp.sum(jnp.where(hit, slot_of[None, :], 0), 1).astype(jnp.int32)
    counts_rows = jnp.sum(jnp.where(hit, tile_counts[None, :], 0), 1).astype(jnp.int32)
    cross_out = steps_major(
        cross_attention(rows_major(q_cross, kv_local), memory, slot_ids, counts_rows, tile_rows)
    )
    return (cross_out, self_out)


def solution(mesh):
    in_specs = (
        P("replica", "pipe", None, "tensor"),
        P(),
        P(),
        P(None, None, "tensor"),
        P("tensor", None),
        P(None, "tensor"),
        P("tensor", None, None),
        P(),
        P(),
        P(("replica", "pipe")),
        P(None, ("replica", "pipe"), "tensor"),
        P(None, ("replica", "pipe"), "tensor"),
        P(("replica", "pipe"), None, None, "tensor"),
        P(None, ("replica", "pipe"), None, "tensor"),
        P(("replica", "pipe")),
    )
    out_specs = (P(None, ("replica", "pipe"), "tensor"), P(None, ("replica", "pipe"), "tensor"))
    return jax.shard_map(shards, mesh=mesh, in_specs=in_specs, out_specs=out_specs, check_vma=False)
```

```python
import functools
import jax
import jax.numpy as jnp
from jax import lax
from jax.experimental import pallas as pl
from jax.experimental.pallas import tpu as pltpu
from jax.sharding import PartitionSpec as P

HEADS = 64
KV_HEADS = 8
HD = 128
ENC_W = 1280
ENC_HEADS = 16
CAP = 2
STEPS = 2
LMAX = 32
NT = (((1,), (1,)), ((), ()))
VMEM_LIMIT = 48 * 1024 * 1024
MESH = pl.DeviceIdType.MESH


def softmax_rows(scores):
    highest = jnp.max(scores, -1, keepdims=True)
    weights = jnp.exp(scores - highest)
    return (weights / jnp.sum(weights, -1, keepdims=True)).astype(jnp.bfloat16)


def peers_of(axis):
    size = lax.axis_size(axis)
    here = lax.axis_index(axis)
    return [(lax.rem(here + d, size), lax.rem(here + size - d, size)) for d in range(1, size)]


def greet(groups):
    barrier = pltpu.get_barrier_semaphore()
    total = 0
    for axis in groups:
        for target, _ in peers_of(axis):
            pl.semaphore_signal(barrier, inc=1, device_id={axis: target}, device_id_type=MESH)
            total += 1
    pl.semaphore_wait(barrier, total)


def route_kernel(
    leaving_ref, lengths_ref, q_ref, kv_ref, whole_ref, self_ref, own_sem, out_send, out_recv,
    side_send, side_recv,
):
    portion = q_ref.shape[0] // leaving_ref.shape[0]
    group = lax.axis_index("replica")
    side = lax.axis_index("tensor")
    greet(("replica", "tensor"))

    def outward(d, target, block):
        return pltpu.make_async_remote_copy(
            src_ref=leaving_ref.at[target], dst_ref=whole_ref.at[side, block],
            send_sem=out_send.at[d], recv_sem=out_recv.at[d],
            device_id={"replica": target}, device_id_type=MESH,
        )

    def sideways(d, step, source, block, target, owner):
        return pltpu.make_async_remote_copy(
            src_ref=source, dst_ref=whole_ref.at[owner, block],
            send_sem=side_send.at[d, step], recv_sem=side_recv.at[d, step],
            device_id={"tensor": target}, device_id_type=MESH,
        )

    others = peers_of("replica")
    sides = peers_of("tensor")
    order = sorted(range(len(others)), key=lambda d: (min(d, len(others) - 1 - d), d))
    for d, (target, _) in enumerate(sides):
        sideways(d, 0, leaving_ref.at[group], group, target, side).start()
    for d in order:
        outward(d, others[d][0], group).start()
    keep = pltpu.make_async_copy(leaving_ref.at[group], whole_ref.at[side, group], own_sem)
    keep.start()

    def decode(index):
        places = [index * portion + r for r in range(portion)]
        self_rows(places, lengths_ref, q_ref, kv_ref, self_ref)

    decode(0)
    for index, d in enumerate(order):
        decode(index + 1)
        block = others[d][1]
        outward(d, others[d][0], block).wait_recv()
        for e, (target, _) in enumerate(sides):
            sideways(e, d + 1, whole_ref.at[side, block], block, target, side).start()
    keep.wait()
    for d in order:
        outward(d, others[d][0], group).wait_send()
    for e, (target, source) in enumerate(sides):
        for step in range(len(others) + 1):
            block = group if step == 0 else others[step - 1][1]
            copy = sideways(e, step, whole_ref.at[side, block], block, target, source)
            copy.wait_recv()
            copy.wait_send()


def route(leaving, lengths, queries, joined):
    replicas = lax.axis_size("replica")
    tensors = lax.axis_size("tensor")
    vmem = pl.BlockSpec(memory_space=pltpu.VMEM)
    return pl.pallas_call(
        route_kernel,
        in_specs=[
            pl.BlockSpec(memory_space=pl.ANY), pl.BlockSpec(memory_space=pltpu.SMEM), vmem, vmem
        ],
        out_specs=(pl.BlockSpec(memory_space=pl.ANY), vmem),
        out_shape=(
            jax.ShapeDtypeStruct((tensors,) + leaving.shape, leaving.dtype),
            jax.ShapeDtypeStruct(queries.shape, jnp.bfloat16),
        ),
        scratch_shapes=[
            pltpu.SemaphoreType.DMA,
            pltpu.SemaphoreType.DMA((replicas - 1,)),
            pltpu.SemaphoreType.DMA((replicas - 1,)),
            pltpu.SemaphoreType.DMA((tensors - 1, replicas)),
            pltpu.SemaphoreType.DMA((tensors - 1, replicas)),
        ],
        compiler_params=pltpu.CompilerParams(
            collective_id=0, has_side_effects=True, vmem_limit_bytes=VMEM_LIMIT
        ),
    )(leaving, lengths, queries, joined)


def project_kernel(rows_ref, gain_ref, weight_ref, query_ref, pair_ref):
    tensors, _, width = rows_ref.shape
    values = [rows_ref[t].astype(jnp.float32) for t in range(tensors)]
    middle = sum(jnp.sum(value, -1, keepdims=True) for value in values) / ENC_W
    centred = [value - middle for value in values]
    spread = sum(jnp.sum(value * value, -1, keepdims=True) for value in centred) / ENC_W
    scale = lax.rsqrt(spread + 1e-06)
    normed = [(value * scale * gain_ref[t]).astype(jnp.bfloat16) for t, value in enumerate(centred)]
    for j in range(3):
        total = sum(
            jnp.dot(
                value, weight_ref[j, t * width : (t + 1) * width, :],
                preferred_element_type=jnp.float32,
            )
            for t, value in enumerate(normed)
        ).astype(jnp.bfloat16)
        if j == 0:
            query_ref[...] = total
        else:
            pair_ref[j - 1] = total


def project(rows, gain, weight):
    tensors, count, part = rows.shape
    width = weight.shape[2]
    block = 256
    return pl.pallas_call(
        project_kernel,
        grid=(count // block,),
        in_specs=[
            pl.BlockSpec((tensors, block, part), lambda i: (0, i, 0)),
            pl.BlockSpec((tensors, 1, part), lambda i: (0, 0, 0)),
            pl.BlockSpec(weight.shape, lambda i: (0, 0, 0)),
        ],
        out_specs=(
            pl.BlockSpec((block, width), lambda i: (i, 0)),
            pl.BlockSpec((2, block, width), lambda i: (0, i, 0)),
        ),
        out_shape=(
            jax.ShapeDtypeStruct((count, width), jnp.bfloat16),
            jax.ShapeDtypeStruct((2, count, width), jnp.bfloat16),
        ),
        compiler_params=pltpu.CompilerParams(vmem_limit_bytes=VMEM_LIMIT),
        cost_estimate=pl.CostEstimate(
            flops=6 * count * ENC_W * width, bytes_accessed=2 * (3 * rows.size + weight.size),
            transcendentals=0,
        ),
    )(rows, gain, weight)


def joint_kernel(
    members_col, proj_ref, out_w_ref, pieces_ref, out_ref, out_rows_ref, rows, leaving, coming,
    row_sem, send, recv, w_send, w_recv,
):
    part_rows, features = rows.shape
    side = lax.axis_index("tensor")
    member = lax.axis_index("replica") * lax.axis_size("pipe") + lax.axis_index("pipe")
    first = pl.multiple_of(member // members_col * part_rows, 8)
    load = pltpu.make_async_copy(proj_ref.at[pl.ds(first, part_rows)], rows, row_sem)
    load.start()
    sides = peers_of("tensor")
    greet(("tensor",))

    def w_copy(d, target):
        return pltpu.make_async_remote_copy(
            src_ref=out_w_ref, dst_ref=out_rows_ref.at[side],
            send_sem=w_send.at[d], recv_sem=w_recv.at[d],
            device_id={"tensor": target}, device_id_type=MESH,
        )

    def sum_copy(d, target):
        return pltpu.make_async_remote_copy(
            src_ref=leaving.at[d], dst_ref=coming.at[d],
            send_sem=send.at[d], recv_sem=recv.at[d],
            device_id={"tensor": target}, device_id_type=MESH,
        )

    def product(target):
        depth = min(1024, features)
        total = jnp.zeros((part_rows, 2 * HD), jnp.float32)
        for low in range(0, features, depth):
            block = pieces_ref[target, :, low : low + depth]
            total += jnp.dot(
                rows[:, low : low + depth], jnp.concatenate([block[0], block[1]], -1),
                preferred_element_type=jnp.float32,
            )
        return total

    for d, (target, _) in enumerate(sides):
        w_copy(d, target).start()
    out_rows_ref[side] = out_w_ref[...]
    load.wait()
    for d, (target, _) in enumerate(sides):
        leaving[d] = product(target).astype(jnp.bfloat16)
        sum_copy(d, target).start()
    total = product(side)
    for d, (target, _) in enumerate(sides):
        sum_copy(d, target).wait_recv()
        total += coming[d].astype(jnp.float32)
    out_ref[...] = total.astype(jnp.bfloat16)
    for d, (target, _) in enumerate(sides):
        sum_copy(d, target).wait_send()
        w_copy(d, target).wait_send()
        w_copy(d, target).wait_recv()


def joint_block(proj, out_w, pieces, members_col, part_rows):
    tensors, _, features, _ = pieces.shape
    vmem = pl.BlockSpec(memory_space=pltpu.VMEM)
    block = (part_rows, 2 * HD)
    one = pltpu.SemaphoreType.DMA((tensors - 1,))
    return pl.pallas_call(
        functools.partial(joint_kernel, members_col),
        in_specs=[pl.BlockSpec(memory_space=pl.ANY), vmem, vmem],
        out_specs=(vmem, vmem),
        out_shape=(
            jax.ShapeDtypeStruct(block, jnp.bfloat16),
            jax.ShapeDtypeStruct((tensors,) + out_w.shape, jnp.bfloat16),
        ),
        scratch_shapes=[
            pltpu.VMEM((part_rows, features), jnp.bfloat16),
            pltpu.VMEM((tensors - 1,) + block, jnp.bfloat16),
            pltpu.VMEM((tensors - 1,) + block, jnp.bfloat16),
            pltpu.SemaphoreType.DMA, one, one, one, one,
        ],
        compiler_params=pltpu.CompilerParams(
            collective_id=3, has_side_effects=True, vmem_limit_bytes=VMEM_LIMIT
        ),
    )(proj, out_w, pieces)


def encoder_kernel(
    head_dim, local_heads, tile_rows, counts_ref, query_ref, pair_ref, joint_ref, out_w_ref,
    rows_ref, gain_ref, memory_ref, joint_all, out_all, pairs, mixed, packed, pair_send, pair_recv,
    side_send, side_recv, last_send, last_recv, own_sem, j_send, j_recv, w_send, w_recv, j_own,
    w_own,
):
    tensors = mixed.shape[0]
    wide = 4
    replicas = joint_ref.shape[0]
    col_parts = joint_all.shape[0]
    pipes, _, slots, rows, width = pairs.shape
    keys = pipes * rows
    per_step = 2
    steps = slots // per_step
    pipe = lax.axis_index("pipe")
    side = lax.axis_index("tensor")
    others = peers_of("pipe")
    sides = peers_of("tensor")
    greet(("pipe", "tensor"))

    def part(step):
        return pl.ds(step * per_step, per_step)

    def pair_copy(d, step, target):
        return pltpu.make_async_remote_copy(
            src_ref=pair_ref.at[:, part(step)], dst_ref=pairs.at[pipe, :, part(step)],
            send_sem=pair_send.at[d, step], recv_sem=pair_recv.at[d, step],
            device_id={"pipe": target}, device_id_type=MESH,
        )

    def side_copy(d, step, target):
        return pltpu.make_async_remote_copy(
            src_ref=mixed.at[side, part(step)], dst_ref=mixed.at[side, part(step)],
            send_sem=side_send.at[d, step], recv_sem=side_recv.at[d, step],
            device_id={"tensor": target}, device_id_type=MESH,
        )

    def broad(step):
        return pl.ds(step * wide, wide)

    def last_copy(d, step, target):
        return pltpu.make_async_remote_copy(
            src_ref=packed.at[broad(step)], dst_ref=memory_ref.at[pipe, broad(step)],
            send_sem=last_send.at[d, step], recv_sem=last_recv.at[d, step],
            device_id={"pipe": target}, device_id_type=MESH,
        )

    def own_copy(step):
        return pltpu.make_async_copy(
            packed.at[broad(step)], memory_ref.at[pipe, broad(step)], own_sem.at[step]
        )

    def place(r):
        member = r * pipes + pipe
        return joint_all.at[member % col_parts, member // col_parts], out_all.at[:, r, pipe]

    def weight_copies(d, r, target):
        joint_spot, out_spot = place(r)
        to = {"pipe": target}
        return (
            pltpu.make_async_remote_copy(
                src_ref=joint_ref.at[r], dst_ref=joint_spot, send_sem=j_send.at[d, r],
                recv_sem=j_recv.at[d, r], device_id=to, device_id_type=MESH,
            ),
            pltpu.make_async_remote_copy(
                src_ref=out_w_ref.at[r], dst_ref=out_spot, send_sem=w_send.at[d, r],
                recv_sem=w_recv.at[d, r], device_id=to, device_id_type=MESH,
            ),
        )

    def weight_keeps(r):
        joint_spot, out_spot = place(r)
        return (
            pltpu.make_async_copy(joint_ref.at[r], joint_spot, j_own.at[r]),
            pltpu.make_async_copy(out_w_ref.at[r], out_spot, w_own.at[r]),
        )

    @pl.loop(0, steps)
    def _(step):
        for d, (target, _) in enumerate(others):
            pair_copy(d, step, target).start()

    @pl.loop(0, replicas)
    def _(r):
        for copy in weight_keeps(r):
            copy.start()
        for d, (target, _) in enumerate(others):
            for copy in weight_copies(d, r, target):
                copy.start()

    lane = lax.broadcasted_iota(jnp.int32, (1, width), 1)
    key_tile = lax.broadcasted_iota(jnp.int32, (1, keys), 1) // tile_rows
    windows = []
    for h in range(0, local_heads, 2):
        low = h * head_dim // 128 * 128
        high = min(-(-(h + 2) * head_dim // 128) * 128, width)
        spots = lane[:, low:high]
        owns = [(spots >= g * head_dim) & (spots < (g + 1) * head_dim) for g in (h, h + 1)]
        windows.append((low, high, owns))

    @pl.loop(0, steps)
    def _(step):
        pairs[pipe, :, part(step)] = pair_ref[:, part(step)]
        for d, (target, _) in enumerate(others):
            pair_copy(d, step, target).wait_recv()
        scores = []
        for s in range(per_step):
            slot = step * per_step + s
            valid = key_tile < counts_ref[slot]
            for low, high, owns in windows:
                plain = query_ref[slot, :, low:high]
                both = [jnp.where(own, plain, jnp.zeros((), jnp.bfloat16)) for own in owns]
                key = pairs[:, 0, slot, :, low:high].reshape(keys, high - low)
                score = lax.dot_general(
                    jnp.concatenate(both, 0), key, NT, preferred_element_type=jnp.float32
                )
                scores.append(jnp.where(valid, score * head_dim ** (-0.5), -1e30))
        probs = [softmax_rows(score) for score in scores]
        results = []
        for s in range(per_step):
            slot = step * per_step + s
            for w, (low, high, _) in enumerate(windows):
                value = pairs[:, 1, slot, :, low:high].reshape(keys, high - low)
                results.append(
                    jnp.dot(
                        probs[s * len(windows) + w], value, preferred_element_type=jnp.float32
                    )
                )
        for s in range(per_step):
            slot = step * per_step + s
            pieces = [None] * (-(-width // 128))
            for w, (low, high, owns) in enumerate(windows):
                result = results[s * len(windows) + w]
                joined = jnp.where(owns[0], result[:rows], jnp.where(owns[1], result[rows:], 0.0))
                for at in range(low // 128, -(-high // 128)):
                    piece = joined[:, at * 128 - low : min((at + 1) * 128, high) - low]
                    pieces[at] = piece if pieces[at] is None else pieces[at] + piece
            for at, piece in enumerate(pieces):
                mixed[side, slot, :, at * 128 : at * 128 + piece.shape[1]] = piece.astype(jnp.bfloat16)
        for d, (target, _) in enumerate(sides):
            side_copy(d, step, target).start()

    kv_width = col_parts * HD

    @pl.loop(0, replicas)
    def _(r):
        for copy in weight_keeps(r):
            copy.wait()
        for d, (target, _) in enumerate(others):
            for copy in weight_copies(d, r, target):
                copy.wait_recv()

    @pl.loop(0, slots // wide)
    def _(step):
        for d, (target, _) in enumerate(sides):
            for half in range(wide // per_step):
                side_copy(d, step * (wide // per_step) + half, target).wait_recv()
        count = wide * rows
        added = sum(
            jnp.dot(
                mixed[t, broad(step)].reshape(count, width), out_all[t].reshape(width, ENC_W),
                preferred_element_type=jnp.float32,
            )
            for t in range(tensors)
        )
        encoded = [
            (
                rows_ref[t, broad(step)].reshape(count, width).astype(jnp.float32)
                + added[:, t * width : (t + 1) * width]
            ).astype(jnp.bfloat16)
            for t in range(tensors)
        ]
        for c in range(col_parts):
            summed = sum(
                jnp.dot(
                    encoded[t], joint_all[c].reshape(ENC_W, 2 * HD)[t * width : (t + 1) * width],
                    preferred_element_type=jnp.float32,
                )
                for t in range(tensors)
            )
            head = summed[:, :HD]
            spread = jnp.mean(head * head, -1, keepdims=True)
            head = head * lax.rsqrt(spread + 1e-05) * gain_ref[...]
            low = c * HD
            packed[broad(step), :, low : low + HD] = head.astype(jnp.bfloat16).reshape(
                wide, rows, HD
            )
            packed[broad(step), :, kv_width + low : kv_width + low + HD] = (
                summed[:, HD:].astype(jnp.bfloat16).reshape(wide, rows, HD)
            )
        for d, (target, _) in enumerate(others):
            last_copy(d, step, target).start()
        own_copy(step).start()

    @pl.loop(0, steps)
    def _(step):
        for d, (target, _) in enumerate(others):
            pair_copy(d, step, target).wait_send()
        for d, (target, _) in enumerate(sides):
            side_copy(d, step, target).wait_send()

    @pl.loop(0, replicas)
    def _(r):
        for d, (target, _) in enumerate(others):
            for copy in weight_copies(d, r, target):
                copy.wait_send()

    @pl.loop(0, slots // wide)
    def _(step):
        for d, (target, _) in enumerate(others):
            last_copy(d, step, target).wait_send()
            last_copy(d, step, target).wait_recv()
        own_copy(step).wait()


def encoder(
    counts, queries, pair, joint, out_w, whole_rows, gain, col_parts, head_dim, tile_rows
):
    slots, rows_image, width = queries.shape
    pipes = lax.axis_size("pipe")
    tensors = lax.axis_size("tensor")
    steps, wide_steps = slots // 2, slots // 4
    replicas, out_rows = joint.shape[0], out_w.shape[2]
    row_parts = replicas * pipes // col_parts
    both = 2 * col_parts * HD
    dma = pltpu.SemaphoreType.DMA
    anywhere = pl.BlockSpec(memory_space=pl.ANY)
    vmem = pl.BlockSpec(memory_space=pltpu.VMEM)
    return pl.pallas_call(
        functools.partial(encoder_kernel, head_dim, width // head_dim, tile_rows),
        in_specs=[
            pl.BlockSpec(memory_space=pltpu.SMEM), vmem, vmem, anywhere, anywhere, vmem, vmem
        ],
        out_specs=anywhere,
        out_shape=jax.ShapeDtypeStruct((pipes, slots, rows_image, both), jnp.bfloat16),
        scratch_shapes=[
            pltpu.VMEM((col_parts, row_parts) + joint.shape[1:], jnp.bfloat16),
            pltpu.VMEM((tensors, replicas, pipes, out_rows, ENC_W), jnp.bfloat16),
            pltpu.VMEM((pipes,) + pair.shape, jnp.bfloat16),
            pltpu.VMEM((tensors, slots, rows_image, width), jnp.bfloat16),
            pltpu.VMEM((slots, rows_image, both), jnp.bfloat16),
            dma((pipes - 1, steps)), dma((pipes - 1, steps)),
            dma((tensors - 1, steps)), dma((tensors - 1, steps)),
            dma((pipes - 1, wide_steps)), dma((pipes - 1, wide_steps)), dma((wide_steps,)),
            dma((pipes - 1, replicas)), dma((pipes - 1, replicas)),
            dma((pipes - 1, replicas)), dma((pipes - 1, replicas)),
            dma((replicas,)), dma((replicas,)),
        ],
        compiler_params=pltpu.CompilerParams(
            collective_id=1, has_side_effects=True, vmem_limit_bytes=VMEM_LIMIT
        ),
    )(counts, queries, pair, joint, out_w, whole_rows, gain)


def decode_rows(query_ref, places, out_ref, held, valids):
    kv_local, queries = query_ref.shape[1:3]
    width = kv_local * HD
    scores = []
    for row, pair, valid in zip(places, held, valids):
        for k in range(kv_local):
            scores.append(
                lax.dot_general(
                    query_ref[row, k], pair[:, k * HD : (k + 1) * HD], NT,
                    preferred_element_type=jnp.float32,
                )
            )
    masked = [
        jnp.where(valids[i // kv_local], piece * HD ** (-0.5), -1e30)
        for i, piece in enumerate(scores)
    ]
    probs = softmax_rows(jnp.concatenate(masked, 0))
    for i, (row, pair) in enumerate(zip(places, held)):
        for k in range(kv_local):
            at = (i * kv_local + k) * queries
            mixed = jnp.dot(
                probs[at : at + queries], pair[:, width + k * HD : width + (k + 1) * HD],
                preferred_element_type=jnp.float32,
            )
            out_ref[row, k] = mixed.astype(jnp.bfloat16)


def cross_kernel(tile_rows, slots_ref, counts_ref, q_ref, kv_ref, out_ref):
    block = q_ref.shape[0]
    pipes, _, rows, both = kv_ref.shape
    keys = pipes * rows
    key_tile = lax.broadcasted_iota(jnp.int32, (1, keys), 1) // tile_rows
    for low in range(0, block, 4):
        places = list(range(low, low + 4))
        spots = [pl.program_id(0) * block + r for r in places]
        held = [kv_ref[:, slots_ref[at]].reshape(keys, both) for at in spots]
        decode_rows(q_ref, places, out_ref, held, [key_tile < counts_ref[at] for at in spots])


def self_rows(places, lengths_ref, q_ref, kv_ref, out_ref):
    queries = q_ref.shape[2]
    shape = (queries, kv_ref.shape[1])
    spot = lax.broadcasted_iota(jnp.int32, shape, 1)
    step = lax.broadcasted_iota(jnp.int32, shape, 0) // (queries // STEPS)
    fresh = (spot >= LMAX) & (spot <= LMAX + step)
    valids = [fresh | (spot < lengths_ref[row]) for row in places]
    decode_rows(q_ref, places, out_ref, [kv_ref[row] for row in places], valids)


def cross_attention(queries, memory, slot_ids, counts, tile_rows):
    rows, kv_local, group, _ = queries.shape
    block = 8
    spec = pl.BlockSpec((block, kv_local, group, HD), lambda i, *_: (i, 0, 0, 0))
    keys = memory.shape[0] * memory.shape[2]
    return pl.pallas_call(
        functools.partial(cross_kernel, tile_rows),
        grid_spec=pltpu.PrefetchScalarGridSpec(
            num_scalar_prefetch=2,
            grid=(rows // block,),
            in_specs=[spec, pl.BlockSpec(memory.shape, lambda i, *_: (0, 0, 0, 0))],
            out_specs=spec,
        ),
        out_shape=jax.ShapeDtypeStruct(queries.shape, jnp.bfloat16),
        compiler_params=pltpu.CompilerParams(vmem_limit_bytes=VMEM_LIMIT),
        cost_estimate=pl.CostEstimate(
            flops=16 * rows * kv_local * group * keys * HD,
            bytes_accessed=2 * (memory.size + 2 * queries.size),
            transcendentals=rows * kv_local * group * keys,
        ),
    )(slot_ids, counts, queries, memory)


def rows_major(queries, kv_local):
    steps, rows, _ = queries.shape
    shaped = queries.reshape(steps, rows, kv_local, -1, HD)
    return shaped.transpose(1, 2, 0, 3, 4).reshape(rows, kv_local, -1, HD)


def steps_major(mixed):
    rows, kv_local, group, _ = mixed.shape
    shaped = mixed.reshape(rows, kv_local, STEPS, group // STEPS, HD)
    return shaped.transpose(2, 0, 1, 3, 4).reshape(STEPS, rows, -1)


def shards(
    patches,
    tile_counts,
    ln_gain,
    enc_qkv,
    enc_out_w,
    proj_w,
    cross_kv_w,
    k_gain,
    plan,
    row_pick,
    q_cross,
    q_self,
    cache_kv,
    new_kv,
    kv_len,
):
    replicas = lax.axis_size("replica")
    pipes = lax.axis_size("pipe")
    tensors = lax.axis_size("tensor")
    group = lax.axis_index("replica")
    member = group * pipes + lax.axis_index("pipe")
    members = replicas * pipes
    images, held_tiles, tile_rows, width_part = patches.shape
    head_dim = ENC_W // ENC_HEADS
    rows_image = held_tiles * tile_rows
    slots = replicas * CAP
    rows = slots * rows_image
    width = enc_qkv.shape[2]
    local_heads = width // head_dim

    destination = plan[:, 0]
    grouped = destination.reshape(replicas, images)
    earlier = jnp.arange(images)[:, None] < jnp.arange(images)[None, :]
    same_dest = grouped[:, :, None] == grouped[:, None, :]
    ranks = jnp.sum((same_dest & earlier[None]).astype(jnp.int32), 1)
    my_dest = lax.dynamic_index_in_dim(grouped, group, 0, keepdims=False)
    my_rank = lax.dynamic_index_in_dim(ranks, group, 0, keepdims=False)
    selector = (my_dest[None, None, :] == jnp.arange(replicas)[:, None, None]) & (
        my_rank[None, None, :] == jnp.arange(CAP)[None, :, None]
    )
    leaving = jnp.sum(selector * jnp.arange(images)[None, None, :], -1).reshape(-1)
    outgoing = jnp.take(
        patches.reshape(images, rows_image, width_part), leaving, axis=0, mode="clip"
    )
    kv_width = cross_kv_w.shape[2] // tensors
    kv_local = kv_width // HD
    row_parts = members // kv_local
    part_rows = ENC_W // row_parts
    pieces = lax.optimization_barrier(
        [
            lax.dynamic_slice_in_dim(
                cross_kv_w, t * kv_width + (member % kv_local) * HD, HD, 2
            )
            for t in range(tensors)
        ]
    )
    out_rows = enc_out_w.shape[0] // members
    out_piece = lax.dynamic_slice_in_dim(enc_out_w, member * out_rows, out_rows, 0)
    joint, out_piece = joint_block(
        proj_w, out_piece, jnp.stack([piece.transpose(1, 0, 2) for piece in pieces]), kv_local,
        part_rows,
    )
    joint_half = lax.all_gather(joint, "replica", axis=0)
    out_half = lax.all_gather(out_piece, "replica", axis=0)

    rows_here = row_pick.shape[0]
    fresh = new_kv.transpose(1, 0, 2, 3).reshape(rows_here, STEPS, 2 * kv_width)
    joined = jnp.concatenate(
        [
            cache_kv.reshape(rows_here, LMAX, 2 * kv_width),
            fresh,
            jnp.zeros((rows_here, 16 - STEPS, 2 * kv_width), jnp.bfloat16),
        ],
        1,
    )
    whole_rows, self_out = route(
        outgoing.reshape(replicas, CAP * rows_image, width_part), kv_len,
        rows_major(q_self, kv_local), joined,
    )
    self_out = steps_major(self_out)

    queries, pair = project(
        whole_rows.reshape(tensors, rows, width_part), ln_gain.reshape(tensors, 1, width_part),
        enc_qkv.transpose(1, 0, 2),
    )
    here = (grouped[:, None, :] == group) & (ranks[:, None, :] == jnp.arange(CAP)[None, :, None])
    slot_counts = jnp.sum(here * tile_counts.reshape(replicas, 1, images), -1).reshape(-1)
    memory = encoder(
        slot_counts.astype(jnp.int32), queries.reshape(slots, rows_image, width),
        pair.reshape(2, slots, rows_image, width), joint_half, out_half,
        whole_rows.reshape(tensors, slots, rows_image, width_part), k_gain.reshape(1, HD),
        kv_local, head_dim, tile_rows,
    )

    mine = (destination == group).astype(jnp.int32)
    count = jnp.sum(mine)
    before = jnp.cumsum(mine) - mine
    wanted = row_pick % count
    hit = (mine[None, :] == 1) & (before[None, :] == wanted[:, None])
    index = jnp.arange(replicas * images, dtype=jnp.int32)
    slot_of = index // images * CAP + ranks.reshape(-1)
    slot_ids = jnp.sum(jnp.where(hit, slot_of[None, :], 0), 1).astype(jnp.int32)
    counts_rows = jnp.sum(jnp.where(hit, tile_counts[None, :], 0), 1).astype(jnp.int32)
    cross_out = steps_major(
        cross_attention(rows_major(q_cross, kv_local), memory, slot_ids, counts_rows, tile_rows)
    )
    return (cross_out, self_out)


def solution(mesh):
    in_specs = (
        P("replica", "pipe", None, "tensor"),
        P(),
        P(),
        P(None, None, "tensor"),
        P("tensor", None),
        P(None, "tensor"),
        P("tensor", None, None),
        P(),
        P(),
        P(("replica", "pipe")),
        P(None, ("replica", "pipe"), "tensor"),
        P(None, ("replica", "pipe"), "tensor"),
        P(("replica", "pipe"), None, None, "tensor"),
        P(None, ("replica", "pipe"), None, "tensor"),
        P(("replica", "pipe")),
    )
    out_specs = (P(None, ("replica", "pipe"), "tensor"), P(None, ("replica", "pipe"), "tensor"))
    return jax.shard_map(shards, mesh=mesh, in_specs=in_specs, out_specs=out_specs, check_vma=False)
```

```python
import functools
import jax
import jax.numpy as jnp
from jax import lax
from jax.experimental import pallas as pl
from jax.experimental.pallas import tpu as pltpu
from jax.sharding import PartitionSpec as P

HEADS = 64
KV_HEADS = 8
HD = 128
ENC_W = 1280
ENC_HEADS = 16
CAP = 2
STEPS = 2
LMAX = 32
NT = (((1,), (1,)), ((), ()))
VMEM_LIMIT = 48 * 1024 * 1024
MESH = pl.DeviceIdType.MESH


def softmax_rows(scores):
    highest = jnp.max(scores, -1, keepdims=True)
    weights = jnp.exp(scores - highest)
    return (weights / jnp.sum(weights, -1, keepdims=True)).astype(jnp.bfloat16)


def peers_of(axis):
    size = lax.axis_size(axis)
    here = lax.axis_index(axis)
    return [(lax.rem(here + d, size), lax.rem(here + size - d, size)) for d in range(1, size)]


def greet(groups):
    barrier = pltpu.get_barrier_semaphore()
    total = 0
    for axis in groups:
        for target, _ in peers_of(axis):
            pl.semaphore_signal(barrier, inc=1, device_id={axis: target}, device_id_type=MESH)
            total += 1
    pl.semaphore_wait(barrier, total)


def route_kernel(
    members_col, leaving_ref, lengths_ref, q_ref, cache_ref, fresh_ref, gain_ref, weight_ref, proj_ref, *refs
):
    tensors = gain_ref.shape[0]
    pieces = refs[:tensors]
    (
        whole_ref, self_ref, query_ref, pair_ref, joint_ref, proj_rows, products, parting, coming,
        own_sem, row_sem, out_send, out_recv, side_send, side_recv, sum_send, sum_recv,
    ) = refs[tensors:]
    part_rows, features = proj_rows.shape
    replicas = leaving_ref.shape[0]
    portion = q_ref.shape[0] // replicas
    group = lax.axis_index("replica")
    side = lax.axis_index("tensor")
    member = group * lax.axis_size("pipe") + lax.axis_index("pipe")
    first = pl.multiple_of(member // members_col * part_rows, 8)
    load = pltpu.make_async_copy(proj_ref.at[pl.ds(first, part_rows)], proj_rows, row_sem)
    load.start()
    sides = peers_of("tensor")
    greet(("replica", "tensor"))

    def shift_of(index):
        half, odd = lax.div(index, 2), lax.rem(index, 2)
        return (half + 1) * (1 - odd) + (replicas - 1 - half) * odd

    def source_of(shift):
        return lax.rem(group + replicas - shift, replicas)

    def outward(shift):
        target = lax.rem(group + shift, replicas)
        return pltpu.make_async_remote_copy(
            src_ref=leaving_ref.at[target], dst_ref=whole_ref.at[side, group],
            send_sem=out_send.at[shift - 1], recv_sem=out_recv.at[shift - 1],
            device_id={"replica": target}, device_id_type=MESH,
        )

    def sideways(d, shift, target, owner):
        block = source_of(shift)
        return pltpu.make_async_remote_copy(
            src_ref=whole_ref.at[side, block], dst_ref=whole_ref.at[owner, block],
            send_sem=side_send.at[d, shift], recv_sem=side_recv.at[d, shift],
            device_id={"tensor": target}, device_id_type=MESH,
        )

    def sum_copy(d, target):
        return pltpu.make_async_remote_copy(
            src_ref=parting.at[d], dst_ref=coming.at[d],
            send_sem=sum_send.at[d], recv_sem=sum_recv.at[d],
            device_id={"tensor": target}, device_id_type=MESH,
        )

    def decode(index):
        places = [index * portion + r for r in range(portion)]
        self_rows(places, lengths_ref, q_ref, cache_ref, fresh_ref, self_ref)

    def project(shift):
        for d, (target, source) in enumerate(sides):
            sideways(d, shift, target, source).wait_recv()
        block = source_of(shift)
        projected = project_rows([whole_ref[t, block] for t in range(tensors)], gain_ref, weight_ref)
        query_ref[block] = projected[0]
        pair_ref[0, block] = projected[1]
        pair_ref[1, block] = projected[2]

    @pl.loop(0, replicas - 1)
    def _(index):
        outward(shift_of(index)).start()

    keep = pltpu.make_async_copy(leaving_ref.at[group], whole_ref.at[side, group], own_sem)
    keep.start()
    keep.wait()
    for d, (target, _) in enumerate(sides):
        sideways(d, 0, target, side).start()
    load.wait()
    depth = min(1024, features)
    for t in range(tensors):
        total = jnp.zeros((part_rows, 2 * HD), jnp.float32)
        for low in range(0, features, depth):
            both = [pieces[t][j, low : low + depth] for j in range(2)]
            total += jnp.dot(
                proj_rows[:, low : low + depth], jnp.concatenate(both, -1),
                preferred_element_type=jnp.float32,
            )
        products[t] = total
    for d, (target, _) in enumerate(sides):
        parting[d] = products[target].astype(jnp.bfloat16)
        sum_copy(d, target).start()

    @pl.loop(0, replicas - 1)
    def _(index):
        shift = shift_of(index)
        outward(shift).wait_recv()
        for d, (target, _) in enumerate(sides):
            sideways(d, shift, target, side).start()
        decode(index)
        some = lax.div(index + replicas - 1, replicas)
        project(shift_of(index - some) * some)

    decode(replicas - 1)
    total = products[side]
    for d, (target, _) in enumerate(sides):
        sum_copy(d, target).wait_recv()
        total += coming[d].astype(jnp.float32)
    joint_ref[...] = total.astype(jnp.bfloat16)
    project(shift_of(replicas - 2))

    @pl.loop(1, replicas)
    def _(shift):
        outward(shift).wait_send()

    for d, (target, _) in enumerate(sides):
        sum_copy(d, target).wait_send()

        @pl.loop(0, replicas)
        def _(shift):
            sideways(d, shift, target, side).wait_send()


def project_rows(parts, gain_ref, weight_ref):
    width = parts[0].shape[1]
    values = [part.astype(jnp.float32) for part in parts]
    middle = sum(jnp.sum(value, -1, keepdims=True) for value in values) / ENC_W
    centred = [value - middle for value in values]
    spread = sum(jnp.sum(value * value, -1, keepdims=True) for value in centred) / ENC_W
    scale = lax.rsqrt(spread + 1e-06)
    normed = [(value * scale * gain_ref[t]).astype(jnp.bfloat16) for t, value in enumerate(centred)]
    return [
        sum(
            jnp.dot(
                value, weight_ref[j, t * width : (t + 1) * width, :],
                preferred_element_type=jnp.float32,
            )
            for t, value in enumerate(normed)
        ).astype(jnp.bfloat16)
        for j in range(3)
    ]


def route(
    leaving, lengths, queries, cache, fresh, gain, weight, proj, pieces, members_col, part_rows
):
    replicas, count, _ = leaving.shape
    tensors = len(pieces)
    features = proj.shape[1]
    width = weight.shape[2]
    vmem = pl.BlockSpec(memory_space=pltpu.VMEM)
    anywhere = pl.BlockSpec(memory_space=pl.ANY)
    block = (part_rows, 2 * HD)
    dma = pltpu.SemaphoreType.DMA
    return pl.pallas_call(
        functools.partial(route_kernel, members_col),
        in_specs=[vmem, pl.BlockSpec(memory_space=pltpu.SMEM)] + [vmem] * 5 + [anywhere]
        + [vmem] * tensors,
        out_specs=(vmem, vmem, vmem, vmem, vmem),
        out_shape=(
            jax.ShapeDtypeStruct((tensors,) + leaving.shape, leaving.dtype),
            jax.ShapeDtypeStruct(queries.shape, jnp.bfloat16),
            jax.ShapeDtypeStruct((replicas, count, width), jnp.bfloat16),
            jax.ShapeDtypeStruct((2, replicas, count, width), jnp.bfloat16),
            jax.ShapeDtypeStruct(block, jnp.bfloat16),
        ),
        scratch_shapes=[
            pltpu.VMEM((part_rows, features), jnp.bfloat16),
            pltpu.VMEM((tensors,) + block, jnp.float32),
            pltpu.VMEM((tensors - 1,) + block, jnp.bfloat16),
            pltpu.VMEM((tensors - 1,) + block, jnp.bfloat16),
            dma, dma, dma((replicas - 1,)), dma((replicas - 1,)),
            dma((tensors - 1, replicas)), dma((tensors - 1, replicas)),
            dma((tensors - 1,)), dma((tensors - 1,)),
        ],
        compiler_params=pltpu.CompilerParams(
            collective_id=0, has_side_effects=True, vmem_limit_bytes=VMEM_LIMIT
        ),
    )(leaving, lengths, queries, cache, fresh, gain, weight, proj, *pieces)


def encoder_kernel(
    head_dim, local_heads, tile_rows, counts_ref, query_ref, pair_ref, joint_ref, out_w_ref,
    rows_ref, gain_ref, memory_ref, joint_all, out_all, pairs, mixed, pair_send, pair_recv,
    side_send, side_recv, last_send, last_recv, j_send, j_recv, w_send, w_recv, w_own,
    far_send, far_recv,
):
    tensors = mixed.shape[0]
    wide = 4
    replicas = out_w_ref.shape[0]
    col_parts = joint_all.shape[0]
    group = lax.axis_index("replica")
    pipes, _, slots, rows, width = pairs.shape
    keys = pipes * rows
    per_step = 2
    steps = slots // per_step
    pipe = lax.axis_index("pipe")
    side = lax.axis_index("tensor")
    others = peers_of("pipe")
    sides = peers_of("tensor")
    far = peers_of("replica")
    far_order = sorted(range(len(far)), key=lambda d: (min(d, len(far) - 1 - d), d))
    greet(("replica", "pipe", "tensor"))

    def part(step):
        return pl.ds(step * per_step, per_step)

    def pair_copy(d, step, target):
        return pltpu.make_async_remote_copy(
            src_ref=pair_ref.at[:, part(step)], dst_ref=pairs.at[pipe, :, part(step)],
            send_sem=pair_send.at[d, step], recv_sem=pair_recv.at[d, step],
            device_id={"pipe": target}, device_id_type=MESH,
        )

    def side_copy(d, step, target):
        return pltpu.make_async_remote_copy(
            src_ref=mixed.at[side, part(step)], dst_ref=mixed.at[side, part(step)],
            send_sem=side_send.at[d, step], recv_sem=side_recv.at[d, step],
            device_id={"tensor": target}, device_id_type=MESH,
        )

    def broad(step):
        return pl.ds(step * wide, wide)

    def last_copy(d, step, target):
        return pltpu.make_async_remote_copy(
            src_ref=memory_ref.at[pipe, broad(step)], dst_ref=memory_ref.at[pipe, broad(step)],
            send_sem=last_send.at[d, step], recv_sem=last_recv.at[d, step],
            device_id={"pipe": target}, device_id_type=MESH,
        )

    def place(r):
        member = r * pipes + pipe
        return joint_all.at[member % col_parts, member // col_parts]

    def joint_out(d, target):
        return pltpu.make_async_remote_copy(
            src_ref=joint_ref, dst_ref=place(group), send_sem=far_send.at[d],
            recv_sem=far_recv.at[d], device_id={"replica": target}, device_id_type=MESH,
        )

    def joint_copy(d, step, r, target):
        return pltpu.make_async_remote_copy(
            src_ref=place(r), dst_ref=place(r), send_sem=j_send.at[d, step],
            recv_sem=j_recv.at[d, step], device_id={"pipe": target}, device_id_type=MESH,
        )

    def weight_copy(d, r, target):
        return pltpu.make_async_remote_copy(
            src_ref=out_w_ref.at[r], dst_ref=out_all.at[:, r, pipe], send_sem=w_send.at[d, r],
            recv_sem=w_recv.at[d, r], device_id={"pipe": target}, device_id_type=MESH,
        )

    def weight_keep(r):
        return pltpu.make_async_copy(out_w_ref.at[r], out_all.at[:, r, pipe], w_own.at[r])

    for d in far_order:
        joint_out(d, far[d][0]).start()
    place(group)[...] = joint_ref[...]

    @pl.loop(0, steps)
    def _(step):
        for d, (target, _) in enumerate(others):
            pair_copy(d, step, target).start()

    for d, (target, _) in enumerate(others):
        joint_copy(d, 0, group, target).start()

    @pl.loop(0, replicas)
    def _(r):
        weight_keep(r).start()
        for d, (target, _) in enumerate(others):
            weight_copy(d, r, target).start()

    lane = lax.broadcasted_iota(jnp.int32, (1, width), 1)
    key_tile = lax.broadcasted_iota(jnp.int32, (1, keys), 1) // tile_rows
    windows = []
    for h in range(0, local_heads, 2):
        low = h * head_dim // 128 * 128
        high = min(-(-(h + 2) * head_dim // 128) * 128, width)
        spots = lane[:, low:high]
        owns = [(spots >= g * head_dim) & (spots < (g + 1) * head_dim) for g in (h, h + 1)]
        windows.append((low, high, owns))

    @pl.loop(0, steps)
    def _(step):
        pairs[pipe, :, part(step)] = pair_ref[:, part(step)]
        for d, (target, _) in enumerate(others):
            pair_copy(d, step, target).wait_recv()
        scores = []
        for s in range(per_step):
            slot = step * per_step + s
            valid = key_tile < counts_ref[slot]
            for low, high, owns in windows:
                plain = query_ref[slot, :, low:high]
                both = [jnp.where(own, plain, jnp.zeros((), jnp.bfloat16)) for own in owns]
                key = pairs[:, 0, slot, :, low:high].reshape(keys, high - low)
                score = lax.dot_general(
                    jnp.concatenate(both, 0), key, NT, preferred_element_type=jnp.float32
                )
                scores.append(jnp.where(valid, score * head_dim ** (-0.5), -1e30))
        probs = [softmax_rows(score) for score in scores]
        results = []
        for s in range(per_step):
            slot = step * per_step + s
            for w, (low, high, _) in enumerate(windows):
                value = pairs[:, 1, slot, :, low:high].reshape(keys, high - low)
                results.append(
                    jnp.dot(
                        probs[s * len(windows) + w], value, preferred_element_type=jnp.float32
                    )
                )
        for s in range(per_step):
            slot = step * per_step + s
            pieces = [None] * (-(-width // 128))
            for w, (low, high, owns) in enumerate(windows):
                result = results[s * len(windows) + w]
                joined = jnp.where(owns[0], result[:rows], jnp.where(owns[1], result[rows:], 0.0))
                for at in range(low // 128, -(-high // 128)):
                    piece = joined[:, at * 128 - low : min((at + 1) * 128, high) - low]
                    pieces[at] = piece if pieces[at] is None else pieces[at] + piece
            for at, piece in enumerate(pieces):
                mixed[side, slot, :, at * 128 : at * 128 + piece.shape[1]] = piece.astype(jnp.bfloat16)
        for d, (target, _) in enumerate(sides):
            side_copy(d, step, target).start()

    kv_width = col_parts * HD

    for d in far_order:
        source = far[d][1]
        joint_out(d, far[d][0]).wait_recv()
        for e, (target, _) in enumerate(others):
            joint_copy(e, d + 1, source, target).start()

    @pl.loop(0, replicas)
    def _(r):
        weight_keep(r).wait()
        for d, (target, _) in enumerate(others):
            weight_copy(d, r, target).wait_recv()

    for step in range(replicas):
        source = group if step == 0 else far[step - 1][1]
        for d, (target, _) in enumerate(others):
            joint_copy(d, step, source, target).wait_recv()

    @pl.loop(0, slots // wide)
    def _(step):
        for d, (target, _) in enumerate(sides):
            for half in range(wide // per_step):
                side_copy(d, step * (wide // per_step) + half, target).wait_recv()
        count = wide * rows
        added = sum(
            jnp.dot(
                mixed[t, broad(step)].reshape(count, width), out_all[t].reshape(width, ENC_W),
                preferred_element_type=jnp.float32,
            )
            for t in range(tensors)
        )
        encoded = [
            (
                rows_ref[t, broad(step)].reshape(count, width).astype(jnp.float32)
                + added[:, t * width : (t + 1) * width]
            ).astype(jnp.bfloat16)
            for t in range(tensors)
        ]
        for c in range(col_parts):
            summed = sum(
                jnp.dot(
                    encoded[t], joint_all[c].reshape(ENC_W, 2 * HD)[t * width : (t + 1) * width],
                    preferred_element_type=jnp.float32,
                )
                for t in range(tensors)
            )
            head = summed[:, :HD]
            spread = jnp.mean(head * head, -1, keepdims=True)
            head = head * lax.rsqrt(spread + 1e-05) * gain_ref[...]
            low = c * HD
            memory_ref[pipe, broad(step), :, low : low + HD] = head.astype(jnp.bfloat16).reshape(
                wide, rows, HD
            )
            memory_ref[pipe, broad(step), :, kv_width + low : kv_width + low + HD] = (
                summed[:, HD:].astype(jnp.bfloat16).reshape(wide, rows, HD)
            )
        for d, (target, _) in enumerate(others):
            last_copy(d, step, target).start()

    @pl.loop(0, steps)
    def _(step):
        for d, (target, _) in enumerate(others):
            pair_copy(d, step, target).wait_send()
        for d, (target, _) in enumerate(sides):
            side_copy(d, step, target).wait_send()

    @pl.loop(0, replicas)
    def _(r):
        for d, (target, _) in enumerate(others):
            weight_copy(d, r, target).wait_send()

    for d in far_order:
        joint_out(d, far[d][0]).wait_send()
    for step in range(replicas):
        source = group if step == 0 else far[step - 1][1]
        for d, (target, _) in enumerate(others):
            joint_copy(d, step, source, target).wait_send()

    @pl.loop(0, slots // wide)
    def _(step):
        for d, (target, _) in enumerate(others):
            last_copy(d, step, target).wait_send()
            last_copy(d, step, target).wait_recv()


def encoder(
    counts, queries, pair, joint, out_w, whole_rows, gain, col_parts, head_dim, tile_rows
):
    slots, rows_image, width = queries.shape
    pipes = lax.axis_size("pipe")
    tensors = lax.axis_size("tensor")
    steps, wide_steps = slots // 2, slots // 4
    replicas, out_rows = out_w.shape[0], out_w.shape[2]
    row_parts = replicas * pipes // col_parts
    both = 2 * col_parts * HD
    dma = pltpu.SemaphoreType.DMA
    anywhere = pl.BlockSpec(memory_space=pl.ANY)
    vmem = pl.BlockSpec(memory_space=pltpu.VMEM)
    return pl.pallas_call(
        functools.partial(encoder_kernel, head_dim, width // head_dim, tile_rows),
        in_specs=[
            pl.BlockSpec(memory_space=pltpu.SMEM), vmem, vmem, vmem, anywhere, vmem, vmem
        ],
        out_specs=vmem,
        out_shape=jax.ShapeDtypeStruct((pipes, slots, rows_image, both), jnp.bfloat16),
        scratch_shapes=[
            pltpu.VMEM((col_parts, row_parts) + joint.shape, jnp.bfloat16),
            pltpu.VMEM((tensors, replicas, pipes, out_rows, ENC_W), jnp.bfloat16),
            pltpu.VMEM((pipes,) + pair.shape, jnp.bfloat16),
            pltpu.VMEM((tensors, slots, rows_image, width), jnp.bfloat16),
            dma((pipes - 1, steps)), dma((pipes - 1, steps)),
            dma((tensors - 1, steps)), dma((tensors - 1, steps)),
            dma((pipes - 1, wide_steps)), dma((pipes - 1, wide_steps)),
            dma((pipes - 1, replicas)), dma((pipes - 1, replicas)),
            dma((pipes - 1, replicas)), dma((pipes - 1, replicas)),
            dma((replicas,)), dma((replicas - 1,)), dma((replicas - 1,)),
        ],
        compiler_params=pltpu.CompilerParams(
            collective_id=1, has_side_effects=True, vmem_limit_bytes=VMEM_LIMIT
        ),
    )(counts, queries, pair, joint, out_w, whole_rows, gain)


def decode_rows(query_ref, places, out_ref, held, valids):
    kv_local, queries = query_ref.shape[1:3]
    width = kv_local * HD
    scores = []
    for row, pair, valid in zip(places, held, valids):
        for k in range(kv_local):
            scores.append(
                lax.dot_general(
                    query_ref[row, k], pair[:, k * HD : (k + 1) * HD], NT,
                    preferred_element_type=jnp.float32,
                )
            )
    masked = [
        jnp.where(valids[i // kv_local], piece * HD ** (-0.5), -1e30)
        for i, piece in enumerate(scores)
    ]
    probs = softmax_rows(jnp.concatenate(masked, 0))
    for i, (row, pair) in enumerate(zip(places, held)):
        for k in range(kv_local):
            at = (i * kv_local + k) * queries
            mixed = jnp.dot(
                probs[at : at + queries], pair[:, width + k * HD : width + (k + 1) * HD],
                preferred_element_type=jnp.float32,
            )
            out_ref[row, k] = mixed.astype(jnp.bfloat16)


def cross_kernel(tile_rows, slots_ref, counts_ref, q_ref, kv_ref, out_ref):
    block = q_ref.shape[0]
    pipes, _, rows, both = kv_ref.shape
    keys = pipes * rows
    key_tile = lax.broadcasted_iota(jnp.int32, (1, keys), 1) // tile_rows
    for low in range(0, block, 4):
        places = list(range(low, low + 4))
        spots = [pl.program_id(0) * block + r for r in places]
        held = [kv_ref[:, slots_ref[at]].reshape(keys, both) for at in spots]
        decode_rows(q_ref, places, out_ref, held, [key_tile < counts_ref[at] for at in spots])


def self_rows(places, lengths_ref, q_ref, cache_ref, fresh_ref, out_ref):
    queries = q_ref.shape[2]
    shape = (queries, cache_ref.shape[1] + fresh_ref.shape[1])
    spot = lax.broadcasted_iota(jnp.int32, shape, 1)
    step = lax.broadcasted_iota(jnp.int32, shape, 0) // (queries // STEPS)
    fresh = (spot >= LMAX) & (spot <= LMAX + step)
    valids = [fresh | (spot < lengths_ref[row]) for row in places]
    held = [jnp.concatenate([cache_ref[row], fresh_ref[row]], 0) for row in places]
    decode_rows(q_ref, places, out_ref, held, valids)


def cross_attention(queries, memory, slot_ids, counts, tile_rows):
    rows, kv_local, group, _ = queries.shape
    block = 8
    spec = pl.BlockSpec((block, kv_local, group, HD), lambda i, *_: (i, 0, 0, 0))
    keys = memory.shape[0] * memory.shape[2]
    return pl.pallas_call(
        functools.partial(cross_kernel, tile_rows),
        grid_spec=pltpu.PrefetchScalarGridSpec(
            num_scalar_prefetch=2,
            grid=(rows // block,),
            in_specs=[spec, pl.BlockSpec(memory.shape, lambda i, *_: (0, 0, 0, 0))],
            out_specs=spec,
        ),
        out_shape=jax.ShapeDtypeStruct(queries.shape, jnp.bfloat16),
        compiler_params=pltpu.CompilerParams(vmem_limit_bytes=VMEM_LIMIT),
        cost_estimate=pl.CostEstimate(
            flops=16 * rows * kv_local * group * keys * HD,
            bytes_accessed=2 * (memory.size + 2 * queries.size),
            transcendentals=rows * kv_local * group * keys,
        ),
    )(slot_ids, counts, queries, memory)


def rows_major(queries, kv_local):
    steps, rows, _ = queries.shape
    shaped = queries.reshape(steps, rows, kv_local, -1, HD)
    return shaped.transpose(1, 2, 0, 3, 4).reshape(rows, kv_local, -1, HD)


def steps_major(mixed):
    rows, kv_local, group, _ = mixed.shape
    shaped = mixed.reshape(rows, kv_local, STEPS, group // STEPS, HD)
    return shaped.transpose(2, 0, 1, 3, 4).reshape(STEPS, rows, -1)


def shards(
    patches,
    tile_counts,
    ln_gain,
    enc_qkv,
    enc_out_w,
    proj_w,
    cross_kv_w,
    k_gain,
    plan,
    row_pick,
    q_cross,
    q_self,
    cache_kv,
    new_kv,
    kv_len,
):
    replicas = lax.axis_size("replica")
    pipes = lax.axis_size("pipe")
    tensors = lax.axis_size("tensor")
    group = lax.axis_index("replica")
    member = group * pipes + lax.axis_index("pipe")
    members = replicas * pipes
    images, held_tiles, tile_rows, width_part = patches.shape
    head_dim = ENC_W // ENC_HEADS
    rows_image = held_tiles * tile_rows
    slots = replicas * CAP
    rows = slots * rows_image
    width = enc_qkv.shape[2]
    local_heads = width // head_dim

    destination = plan[:, 0]
    grouped = destination.reshape(replicas, images)
    earlier = jnp.arange(images)[:, None] < jnp.arange(images)[None, :]
    same_dest = grouped[:, :, None] == grouped[:, None, :]
    ranks = jnp.sum((same_dest & earlier[None]).astype(jnp.int32), 1)
    my_dest = lax.dynamic_index_in_dim(grouped, group, 0, keepdims=False)
    my_rank = lax.dynamic_index_in_dim(ranks, group, 0, keepdims=False)
    selector = (my_dest[None, None, :] == jnp.arange(replicas)[:, None, None]) & (
        my_rank[None, None, :] == jnp.arange(CAP)[None, :, None]
    )
    leaving = jnp.sum(selector * jnp.arange(images)[None, None, :], -1).reshape(-1)
    outgoing = jnp.take(
        patches.reshape(images, rows_image, width_part), leaving, axis=0, mode="clip"
    )
    kv_width = cross_kv_w.shape[2] // tensors
    kv_local = kv_width // HD
    row_parts = members // kv_local
    part_rows = ENC_W // row_parts
    pieces = lax.optimization_barrier(
        [
            lax.dynamic_slice_in_dim(
                cross_kv_w, t * kv_width + (member % kv_local) * HD, HD, 2
            )
            for t in range(tensors)
        ]
    )
    pieces = [piece.transpose(1, 0, 2) for piece in pieces]
    out_rows = enc_out_w.shape[0] // members
    out_piece = lax.dynamic_slice_in_dim(enc_out_w, member * out_rows, out_rows, 0)
    out_half = lax.all_gather(out_piece, ("replica", "tensor"), axis=0)
    out_half = out_half.reshape(replicas, tensors, out_rows, ENC_W)

    rows_here = row_pick.shape[0]
    fresh = new_kv.transpose(1, 0, 2, 3).reshape(rows_here, STEPS, 2 * kv_width)
    fresh = jnp.pad(fresh, ((0, 0), (0, 16 - STEPS), (0, 0)))
    cache = cache_kv.reshape(rows_here, LMAX, 2 * kv_width)
    whole_rows, self_out, queries, pair, joint = route(
        outgoing.reshape(replicas, CAP * rows_image, width_part), kv_len,
        rows_major(q_self, kv_local), cache, fresh, ln_gain.reshape(tensors, 1, width_part),
        enc_qkv.transpose(1, 0, 2), proj_w, pieces, kv_local, part_rows,
    )
    self_out = steps_major(self_out)

    here = (grouped[:, None, :] == group) & (ranks[:, None, :] == jnp.arange(CAP)[None, :, None])
    slot_counts = jnp.sum(here * tile_counts.reshape(replicas, 1, images), -1).reshape(-1)
    memory = encoder(
        slot_counts.astype(jnp.int32), queries.reshape(slots, rows_image, width),
        pair.reshape(2, slots, rows_image, width), joint, out_half,
        whole_rows.reshape(tensors, slots, rows_image, width_part), k_gain.reshape(1, HD),
        kv_local, head_dim, tile_rows,
    )

    mine = (destination == group).astype(jnp.int32)
    count = jnp.sum(mine)
    before = jnp.cumsum(mine) - mine
    wanted = row_pick % count
    hit = (mine[None, :] == 1) & (before[None, :] == wanted[:, None])
    index = jnp.arange(replicas * images, dtype=jnp.int32)
    slot_of = index // images * CAP + ranks.reshape(-1)
    slot_ids = jnp.sum(jnp.where(hit, slot_of[None, :], 0), 1).astype(jnp.int32)
    counts_rows = jnp.sum(jnp.where(hit, tile_counts[None, :], 0), 1).astype(jnp.int32)
    cross_out = steps_major(
        cross_attention(rows_major(q_cross, kv_local), memory, slot_ids, counts_rows, tile_rows)
    )
    return (cross_out, self_out)


def solution(mesh):
    in_specs = (
        P("replica", "pipe", None, "tensor"),
        P(),
        P(),
        P(None, None, "tensor"),
        P("tensor", None),
        P(None, "tensor"),
        P("tensor", None, None),
        P(),
        P(),
        P(("replica", "pipe")),
        P(None, ("replica", "pipe"), "tensor"),
        P(None, ("replica", "pipe"), "tensor"),
        P(("replica", "pipe"), None, None, "tensor"),
        P(None, ("replica", "pipe"), None, "tensor"),
        P(("replica", "pipe")),
    )
    out_specs = (P(None, ("replica", "pipe"), "tensor"), P(None, ("replica", "pipe"), "tensor"))
    return jax.shard_map(shards, mesh=mesh, in_specs=in_specs, out_specs=out_specs, check_vma=False)
```
